32 devices in a mesh: rep: 8 (over y, x, core), shard: 4 (over z).
Axes of the slice: x: 2, y: 2, z: 4, core: 2. Of those that a mesh axis runs over, the one named last changes fastest.
Arguments:
- token_pool: bfloat16 [8, 384, 2048], P('rep'), may hold values from -6 to 6
- row_index: int32 [8, 2, 1, 512], P('rep'), may hold values from 0 to 383
- weights: bfloat16 [1, 2048, 1024], P(None, None, 'shard'), may hold values from -4 to 4
- targets: bfloat16 [8, 1, 512, 1024], P('rep', None, None, 'shard'), may hold values from -2 to 2
Outputs:
- new_weights: bfloat16 [1, 2048, 1024], P(None, None, 'shard')
The draws below stay inside these ranges and needn't reach their ends.
All inputs are finite; a program needn't handle non-finite values.
Results may differ from the reference program's by a relative error of at most 0.013.
Values may be sent and summed in bfloat16 or wider, within the bound.
No kernel may reach another device: no remote copies, remote signals or barrier semaphores. Data moves between devices by JAX's collectives and lax.ppermute only.
A program may use at most 64 MiB of HBM per device.

```python
import math
import jax
import jax.numpy as jnp
from jax import lax

D = 2048
FF = 512
ROWS = 128
POOL = 384
STEPS = 4
EXP_LOCAL = 1
REPLICAS = 8
LEVELS = 3
BLOCKS = 2


def draw_token_pool(key, part):
    key = jax.random.fold_in(key, 11)
    sign_key, amp_key, column_key, size_key, noise_key = jax.random.split(key, 5)
    place = jnp.arange(D, dtype=jnp.float32) / (D - 1.0)
    odd_column = (jnp.arange(D, dtype=jnp.int32) % 2 == 1).astype(jnp.float32)
    order = jax.random.permutation(sign_key, REPLICAS)
    replica_sign = jnp.where(order < REPLICAS // 2, 1.0, -1.0).astype(jnp.float32)
    replica_amp = jnp.exp(jax.random.uniform(amp_key, (REPLICAS,), jnp.float32, -0.5, 0.5))
    column_sign = jnp.where(jax.random.bernoulli(column_key, 0.5, (D,)), 1.0, -1.0).astype(jnp.float32)
    column_size = jax.random.uniform(size_key, (D,), jnp.float32, 0.5, 1.5)
    offset = odd_column * column_sign * column_size * jnp.sqrt(24.0 / D)
    ramp = 0.4 * jnp.exp(place * 1.609438)
    values = jax.random.normal(noise_key, (REPLICAS, POOL, D), jnp.float32)
    spread = odd_column * 0.3 + (1.0 - odd_column) * ramp
    shifted = (replica_sign * replica_amp)[:, None, None] * offset[None, None, :]
    return jnp.clip(shifted + values * spread[None, None, :], -6.0, 6.0).astype(jnp.bfloat16)


def draw_targets(key, part):
    key = jax.random.fold_in(key, 23)
    sign_key, size_key, noise_key = jax.random.split(key, 3)
    columns = BLOCKS * FF
    column_sign = jnp.where(jax.random.bernoulli(sign_key, 0.5, (columns,)), 1.0, -1.0).astype(jnp.float32)
    column_bias = column_sign * jax.random.uniform(size_key, (columns,), jnp.float32, 0.3, 0.8)
    shape = (REPLICAS, EXP_LOCAL, STEPS * ROWS, columns)
    noise = 0.3 * jax.random.normal(noise_key, shape, jnp.float32)
    return jnp.clip(column_bias[None, None, None, :] + noise, -2.0, 2.0).astype(jnp.bfloat16)


def place_ends(values, stream_key, smallest, high):
    extent = values.shape
    index_at = [jax.random.randint(jax.random.fold_in(stream_key, axis), (), 0, extent[axis]) for axis in range(len(extent))]
    values = values.at[tuple(index_at)].set(smallest)
    longest = extent.index(max(extent))
    index_at[longest] = (index_at[longest] + 1) % extent[longest]
    return values.at[tuple(index_at)].set(high)


def block_levels(own_key, dims, cuts, least, largest):
    level, own = 1.0, jax.random.fold_in(own_key, 6)
    for position, parts in cuts:
        draws = jnp.exp(jax.random.uniform(jax.random.fold_in(own, position), (parts,), jnp.float32, least / len(cuts), largest / len(cuts)))
        level = level * jnp.repeat(draws, dims[position] // parts).reshape([-1 if axis == position else 1 for axis in range(len(dims))])
    return level


def centred(own_key, shape, scale, limit, cuts=(), kind=jnp.bfloat16):
    gain = block_levels(own_key, shape, cuts, -0.22, 0.18) if cuts else 1.0
    values = jax.random.normal(own_key, shape, jnp.float32) * scale * gain
    return jnp.minimum(jnp.maximum(values, -limit), limit).astype(kind)


def setup_inputs(seed: int = 0) -> dict:
    streams_of = jax.random.split(jax.random.key(seed), 5)
    return {
        "token_pool": draw_token_pool(jax.random.fold_in(streams_of[4], 71), 0),
        "row_index": place_ends(jax.random.randint(streams_of[1], (REPLICAS, BLOCKS, EXP_LOCAL, STEPS * ROWS), 0, POOL), jax.random.fold_in(streams_of[1], 1), 0, POOL - 1).astype(jnp.int32),
        "weights": centred(streams_of[2], (EXP_LOCAL, D, BLOCKS * FF), 1.0, 4.0, ((2, 4),)),
        "targets": draw_targets(jax.random.fold_in(streams_of[4], 71), 0),
    }


LEARN_RATE = 0.3
MOMENTUM = 0.9
EPSILON = 1e-06

def local_steps(pool_rows, indices, goals, start_weights):
    running = start_weights.astype(jnp.float32)
    velocity = jnp.zeros_like(running)
    inv_width = 1.0 / math.sqrt(pool_rows.shape[1])
    batch_rows = indices.shape[0] // STEPS
    inv_batch = 1.0 / math.sqrt(batch_rows)
    for step_index in range(STEPS):
        picked = indices[step_index * batch_rows:(step_index + 1) * batch_rows]
        inputs = jnp.take(pool_rows, picked, axis=0)
        wanted = goals[step_index * batch_rows:(step_index + 1) * batch_rows].astype(jnp.float32)
        hidden = jnp.dot(inputs, running.astype(jnp.bfloat16), preferred_element_type=jnp.float32) * inv_width
        sigma = jax.nn.sigmoid(hidden)
        slope = sigma * (1.0 + hidden * (1.0 - sigma))
        grad_hidden = ((hidden * sigma - wanted) * slope).astype(jnp.bfloat16)
        gradient = jnp.dot(inputs.T, grad_hidden, preferred_element_type=jnp.float32) * inv_batch
        velocity = MOMENTUM * velocity + gradient
        running = running - LEARN_RATE * velocity
    return (running - start_weights.astype(jnp.float32)).astype(jnp.bfloat16)

def adasum_tree(deltas):
    current = deltas.astype(jnp.float32)
    for level_index in range(LEVELS):
        pair_count = current.shape[0] // 2
        paired = current.reshape((pair_count, 2) + current.shape[1:])
        left_wide = paired[:, 0]
        right_wide = paired[:, 1]
        cross = lax.optimization_barrier(jnp.sum(left_wide * right_wide, axis=(1, 2)))
        left_square = lax.optimization_barrier(jnp.sum(left_wide * left_wide, axis=(1, 2)))
        right_square = lax.optimization_barrier(jnp.sum(right_wide * right_wide, axis=(1, 2)))
        left_coef = 1.0 - cross / (2.0 * (left_square + EPSILON))
        right_coef = 1.0 - cross / (2.0 * (right_square + EPSILON))
        current = left_coef[:, None, None] * left_wide + right_coef[:, None, None] * right_wide
    return current[0].astype(jnp.bfloat16)

def reference(token_pool, row_index, weights, targets):
    per_slot = []
    for expert_slot in range(EXP_LOCAL):
        block_parts = []
        for block_index in range(BLOCKS):
            start_weights = weights[expert_slot, :, block_index * FF:(block_index + 1) * FF]
            goals = targets[:, expert_slot, :, block_index * FF:(block_index + 1) * FF]
            deltas = jax.vmap(local_steps, in_axes=(0, 0, 0, None))(token_pool, row_index[:, block_index, expert_slot], goals, start_weights)
            combined = adasum_tree(deltas)
            block_parts.append((start_weights.astype(jnp.float32) + combined.astype(jnp.float32)).astype(jnp.bfloat16))
        per_slot.append(jnp.concatenate(block_parts, axis=1))
    return jnp.stack(per_slot, 0)
```

```python
import math

import jax
import jax.numpy as jnp
from jax import lax
from jax.experimental import pallas as pl
from jax.experimental.pallas import tpu as pltpu
from jax.sharding import PartitionSpec as P

FF = 512
STEPS = 4
LEARN_RATE = 0.3
MOMENTUM = 0.9
EPSILON = 1e-06
LOADS = 4
LATE = 3
VMEM_LIMIT = 48 * 1024 * 1024

F32 = jnp.float32
BF16 = jnp.bfloat16


def reach(steps_between):
    return LEARN_RATE * sum(MOMENTUM**k for k in range(steps_between))


def contract(a, b, dims):
    return lax.dot_general(a, b, (dims, ((), ())), preferred_element_type=F32)


def local_kernel(cut, idx_hbm, pool_hbm, w_hbm, goal_hbm, *rest):
    outs, own_ref = rest[:-7], rest[-7]
    idx_ref, pool_ref, w_ref, goal_ref, x_ref, sems = rest[-6:]
    parts = len(outs)
    pool_rows, width = pool_ref.shape
    total_rows = idx_ref.shape[-1]
    batch = total_rows // STEPS
    seg = width // parts
    inv_width = 1.0 / math.sqrt(width)
    inv_batch = 1.0 / math.sqrt(batch)
    share = width // LOADS
    pieces = [pl.ds(n * share, share) for n in range(LOADS)]

    idx_load = pltpu.make_async_copy(
        idx_hbm.at[lax.axis_index("shard") // cut], idx_ref, sems.at[len(pieces) + 2]
    )
    idx_load.start()
    pool_loads = []
    for n in range(LOADS):
        rows = pl.ds(n * (pool_rows // LOADS), pool_rows // LOADS)
        load = pltpu.make_async_copy(pool_hbm.at[rows], pool_ref.at[rows], sems.at[n])
        load.start()
        pool_loads.append(load)
    w_load = pltpu.make_async_copy(w_hbm, w_ref, sems.at[len(pieces)])
    goal_load = pltpu.make_async_copy(goal_hbm, goal_ref, sems.at[len(pieces) + 1])

    idx_load.wait()
    place = lax.broadcasted_iota(jnp.int32, (batch, pool_rows), 1)
    hits = []
    for t in range(STEPS):
        picked = jnp.broadcast_to(idx_ref[:, t * batch : (t + 1) * batch], (8, batch))
        picked = picked.astype(F32).T[:, :1].astype(jnp.int32)
        hits.append(jnp.where(place == picked, 1.0, 0.0).astype(BF16))
    one_hot = jnp.concatenate(hits, axis=0)
    pool_loads[0].wait()
    w_load.start()
    goal_load.start()
    for load in pool_loads[1:]:
        load.wait()
    for piece in pieces:
        x_ref[:, piece] = jnp.dot(
            one_hot, pool_ref[:, piece], preferred_element_type=F32
        ).astype(BF16)
    w_load.wait()
    goal_load.wait()
    base = jnp.dot(x_ref[...], w_ref[...], preferred_element_type=F32) * inv_width

    overlaps = {}
    for s in range(0, STEPS - 1, 2):
        stop = min(s + 2, STEPS - 1)
        overlaps[s] = contract(
            x_ref[(s + 1) * batch :, :], x_ref[s * batch : stop * batch, :], ((1,), (1,))
        )

    spread = []
    for s in range(STEPS - 1):
        first = s // 2 * 2
        halves = []
        for t in range(s + 1, STEPS):
            down, across = (t - first - 1) * batch, (s - first) * batch
            block = overlaps[first][down : down + batch, across : across + batch]
            block = block * (reach(t - s) * inv_batch * inv_width)
            high = block.astype(BF16)
            halves += [high, (block - high.astype(F32)).astype(BF16)]
        spread.append(jnp.concatenate(halves, axis=0))

    hidden = [base[t * batch : (t + 1) * batch] for t in range(STEPS)]
    final = []
    for s in range(STEPS):
        sigma = jax.nn.sigmoid(hidden[s])
        wanted = goal_ref[s * batch : (s + 1) * batch, :].astype(F32)
        grad = (hidden[s] * sigma - wanted) * (sigma * (1.0 + hidden[s] * (1.0 - sigma)))
        if s < STEPS - 1:
            moved = jnp.dot(spread[s], grad.astype(BF16), preferred_element_type=F32)
            for n, t in enumerate(range(s + 1, STEPS)):
                at = 2 * n * batch
                hidden[t] = hidden[t] - (
                    moved[at : at + batch] + moved[at + batch : at + 2 * batch]
                )
        final.append((grad * (-reach(STEPS - s) * inv_batch)).T.astype(BF16))

    turned = jnp.concatenate(final, axis=1)
    me = lax.axis_index("rep")
    own_ref[...] = w_ref[pl.ds(pl.multiple_of(me * seg, seg), seg), :]
    for distance, out_ref in zip(distances(parts), outs):
        target = me ^ distance
        held = max(seg, 128)
        at = pl.multiple_of(target * seg // held * held, held)
        moved = jnp.dot(turned, x_ref[:, pl.ds(at, held)], preferred_element_type=F32)
        share = moved[:, :seg]
        for place in range(1, held // seg):
            own = target % (held // seg) == place
            share = jnp.where(own, moved[:, place * seg : (place + 1) * seg], share)
        out_ref[...] = share.astype(BF16)


def distances(parts):
    def far(distance):
        return (distance == 1, distance & 1, -(distance >> 1).bit_count(), distance)

    return [0, *sorted(range(1, parts), key=far)]


def pair_list(count):
    return [(i, j) for i in range(count) for j in range(i, count)]


def gram_kernel(order, known, *refs):
    count = len(order)
    deltas, before, out_ref = refs[:count], refs[count:-1], refs[-1]
    rows, seg = deltas[0].shape
    lanes = min(128, seg)
    block = min(8, count)
    tall = 16
    me = lax.axis_index("rep")
    down = lax.broadcasted_iota(jnp.int32, out_ref.shape, 0)
    across = lax.broadcasted_iota(jnp.int32, out_ref.shape, 1)
    table = before[0][...] if before else jnp.zeros(out_ref.shape, F32)
    for first in range(0, count, block):
        for second in range(first, count, block):
            pairs = [
                (i, j)
                for i in range(first, min(first + block, count))
                for j in range(second, min(second + block, count))
                if i <= j and j >= known
            ]
            if not pairs:
                continue
            members = sorted({k for pair in pairs for k in pair})

            def step(at, sums, pairs=pairs, members=members):
                sums = list(sums)
                row = pl.multiple_of(at * tall, tall)
                for lane in range(0, seg, lanes):
                    held = {
                        k: deltas[k][pl.ds(row, tall), lane : lane + lanes].astype(F32)
                        for k in members
                    }
                    for n, (i, j) in enumerate(pairs):
                        product = held[i] * held[j]
                        sums[n] = sums[n] + (product[:8] + product[8:])
                return tuple(sums)

            zeros = tuple(jnp.zeros((8, lanes), F32) for _ in pairs)
            sums = lax.fori_loop(0, rows // tall, step, zeros)
            for n, (i, j) in enumerate(pairs):
                value = jnp.sum(jnp.sum(sums[n], axis=0, keepdims=True), axis=1, keepdims=True)
                mine, other = me ^ order[i], me ^ order[j]
                spot = ((down == mine) & (across == other)) | ((down == other) & (across == mine))
                table = jnp.where(spot, value, table)
    out_ref[...] = table


def tree_weights(gram, count):
    weights = [None] * count
    current = dict(gram)
    width = 1
    while count > 1:
        left, right = [], []
        for i in range(0, count, 2):
            cross = current[i, i + 1]
            left_square = jnp.maximum(current[i, i], 0.0)
            right_square = jnp.maximum(current[i + 1, i + 1], 0.0)
            left.append(1.0 - cross / (2.0 * (left_square + EPSILON)))
            right.append(1.0 - cross / (2.0 * (right_square + EPSILON)))
        for i in range(count):
            scale = (right if i % 2 else left)[i // 2]
            for k in range(i * width, (i + 1) * width):
                weights[k] = scale if weights[k] is None else weights[k] * scale
        merged = {}
        for i in range(count // 2):
            for j in range(i, count // 2):

                def entry(a, b):
                    return current[min(a, b), max(a, b)]

                merged[i, j] = left[i] * (
                    left[j] * entry(2 * i, 2 * j) + right[j] * entry(2 * i, 2 * j + 1)
                ) + right[i] * (
                    left[j] * entry(2 * i + 1, 2 * j) + right[j] * entry(2 * i + 1, 2 * j + 1)
                )
        current = merged
        count //= 2
        width *= 2
    return weights


def combine_kernel(gram_ref, own_ref, *rest):
    deltas, out_ref = rest[:-1], rest[-1]
    count = len(deltas)
    me = lax.axis_index("rep")
    table = gram_ref[0]
    for member in range(1, gram_ref.shape[0]):
        table = table + gram_ref[member]
    gram = {(i, j): table[i : i + 1, j : j + 1] for i, j in pair_list(count)}
    weights = tree_weights(gram, count)
    total = None
    for distance, delta in zip(distances(count), deltas):
        weight = weights[0]
        for k in range(1, count):
            weight = jnp.where((me ^ distance) == k, weights[k], weight)
        term = weight * delta[...].astype(F32)
        total = term if total is None else total + term
    combined = total.T.astype(BF16).astype(F32)
    out_ref[...] = (own_ref[...].astype(F32) + combined).astype(BF16)


def place_kernel(*refs):
    pieces, (out_ref, sems) = refs[:-2], refs[-2:]
    seg = pieces[0].shape[0]
    me = lax.axis_index("rep")
    moves = []
    for distance, piece in enumerate(pieces):
        at = pl.multiple_of((me ^ distance) * seg, seg)
        move = pltpu.make_async_copy(piece, out_ref.at[pl.ds(at, seg)], sems.at[distance])
        move.start()
        moves.append(move)
    for move in moves:
        move.wait()


def call(kernel, out_shape, in_specs, scratch=(), out_specs=None):
    extra = {} if out_specs is None else {"out_specs": out_specs}
    return pl.pallas_call(
        kernel,
        out_shape=out_shape,
        in_specs=in_specs,
        scratch_shapes=scratch,
        compiler_params=pltpu.CompilerParams(vmem_limit_bytes=VMEM_LIMIT),
        **extra,
    )


def hold(value):
    return pltpu.with_memory_space_constraint(value, pltpu.HBM)


def flipped(value, replica_bits, shard_bits=0):
    replicas, shards = lax.axis_size("rep"), lax.axis_size("shard")
    pairs = [
        (i * shards + j, (i ^ replica_bits) * shards + (j ^ shard_bits))
        for i in range(replicas)
        for j in range(shards)
    ]
    return lax.ppermute(value, ("rep", "shard"), pairs)


def body(token_pool, row_index, weights, targets):
    parts = lax.axis_size("rep")
    width, columns = weights.shape[1:]
    cut = FF // columns
    seg = width // parts
    rows = row_index.shape[-1]
    pool_rows = token_pool.shape[1]
    near = pl.BlockSpec(memory_space=pltpu.VMEM)
    far = pl.BlockSpec(memory_space=pltpu.HBM)
    any_place = pl.BlockSpec(memory_space=pl.ANY)

    def local(*refs):
        local_kernel(cut, *refs)

    order = distances(parts)
    *sent, own_weights = call(
        local,
        [jax.ShapeDtypeStruct((columns, seg), BF16)] * parts
        + [jax.ShapeDtypeStruct((seg, columns), BF16)],
        [far] * 4,
        [
            pltpu.VMEM((1, rows), jnp.int32),
            pltpu.VMEM((pool_rows, width), BF16),
            pltpu.VMEM((width, columns), BF16),
            pltpu.VMEM((rows, columns), BF16),
            pltpu.VMEM((rows, width), BF16),
            pltpu.SemaphoreType.DMA((LOADS + 3,)),
        ],
    )(hold(row_index[0]), hold(token_pool[0]), hold(weights[0]), hold(targets[0, 0]))
    deltas = [value if d == 0 else flipped(value, d) for d, value in zip(order, sent)]

    tall = -(-parts // 8) * 8
    table = jax.ShapeDtypeStruct((tall, 128), F32)
    late = LATE if parts > LATE + 1 else 0
    soon = order[: parts - late]
    leaves = dict(zip(order, deltas))

    def first_gram(*refs):
        gram_kernel(soon, 0, *refs)

    def full_gram(*refs):
        gram_kernel(order, len(soon), *refs)

    gram = call(first_gram, table, [near] * len(soon))(*(leaves[d] for d in soon))
    if late:
        gram = call(full_gram, table, [near] * (parts + 1))(
            *(leaves[d] for d in order), gram
        )
    shards = lax.axis_size("shard")
    groups = [
        [i * shards + j for i in range(parts) for j in range(first, first + cut)]
        for first in range(0, shards, cut)
    ]
    groups = [group[::-1] for group in groups]
    gram = jnp.broadcast_to(gram, (parts * cut, *gram.shape))
    gram = lax.all_to_all(gram, ("rep", "shard"), 0, 0, axis_index_groups=groups)

    own = call(
        combine_kernel,
        jax.ShapeDtypeStruct((seg, columns), BF16),
        [near] * (parts + 2),
    )(gram, own_weights, *deltas)
    pieces = [own] + [None] * (parts - 1)
    pieces[1] = flipped(own, 1)
    for d in range(2, parts, 2):
        pieces[d + 1] = flipped(own, d + 1)
        pieces[d] = flipped(pieces[d + 1], 1)
    placed = call(
        place_kernel,
        jax.ShapeDtypeStruct((width, columns), BF16),
        [any_place] * parts,
        [pltpu.SemaphoreType.DMA((parts,))],
        far,
    )(*pieces)
    return placed[None]


def solution(mesh):
    in_specs = (
        P("rep", None, None),
        P("rep", None, None, None),
        P(None, None, "shard"),
        P("rep", None, None, "shard"),
    )
    out_specs = P(None, None, "shard")
    return jax.shard_map(body, mesh=mesh, in_specs=in_specs, out_specs=out_specs, check_vma=False)
```

```python
import math

import jax
import jax.numpy as jnp
from jax import lax
from jax.experimental import pallas as pl
from jax.experimental.pallas import tpu as pltpu
from jax.sharding import PartitionSpec as P

FF = 512
STEPS = 4
LEARN_RATE = 0.3
MOMENTUM = 0.9
EPSILON = 1e-06
LOADS = 4
LATE = 3
VMEM_LIMIT = 48 * 1024 * 1024

F32 = jnp.float32
BF16 = jnp.bfloat16


def reach(steps_between):
    return LEARN_RATE * sum(MOMENTUM**k for k in range(steps_between))


def contract(a, b, dims):
    return lax.dot_general(a, b, (dims, ((), ())), preferred_element_type=F32)


def share_rows(turned_ref, x_ref, distance, out_ref):
    seg = out_ref.shape[1]
    target = lax.axis_index("rep") ^ distance
    held = max(seg, 128)
    at = pl.multiple_of(target * seg // held * held, held)
    moved = jnp.dot(turned_ref[...], x_ref[:, pl.ds(at, held)], preferred_element_type=F32)
    share = moved[:, :seg]
    for place in range(1, held // seg):
        own = target % (held // seg) == place
        share = jnp.where(own, moved[:, place * seg : (place + 1) * seg], share)
    out_ref[...] = share.astype(BF16)


def share_kernel(order, turned_ref, x_ref, *rest):
    for distance, out_ref in zip(order, rest[-len(order) :]):
        share_rows(turned_ref, x_ref, distance, out_ref)


def local_kernel(cut, partner, idx_hbm, pool_hbm, w_hbm, goal_hbm, *rest):
    first_ref, own_ref, turned_ref, x_ref = rest[:4]
    idx_ref, pool_ref, w_ref, goal_ref, sems = rest[4:]
    pool_rows, width = pool_ref.shape
    seg = own_ref.shape[0]
    total_rows = idx_ref.shape[-1]
    batch = total_rows // STEPS
    inv_width = 1.0 / math.sqrt(width)
    inv_batch = 1.0 / math.sqrt(batch)
    share = width // LOADS
    pieces = [pl.ds(n * share, share) for n in range(LOADS)]

    idx_load = pltpu.make_async_copy(
        idx_hbm.at[lax.axis_index("shard") // cut], idx_ref, sems.at[len(pieces) + 2]
    )
    idx_load.start()
    pool_loads = []
    for n in range(LOADS):
        rows = pl.ds(n * (pool_rows // LOADS), pool_rows // LOADS)
        load = pltpu.make_async_copy(pool_hbm.at[rows], pool_ref.at[rows], sems.at[n])
        load.start()
        pool_loads.append(load)
    w_load = pltpu.make_async_copy(w_hbm, w_ref, sems.at[len(pieces)])
    goal_load = pltpu.make_async_copy(goal_hbm, goal_ref, sems.at[len(pieces) + 1])

    idx_load.wait()
    place = lax.broadcasted_iota(jnp.int32, (batch, pool_rows), 1)
    hits = []
    for t in range(STEPS):
        picked = jnp.broadcast_to(idx_ref[:, t * batch : (t + 1) * batch], (8, batch))
        picked = picked.astype(F32).T[:, :1].astype(jnp.int32)
        hits.append(jnp.where(place == picked, 1.0, 0.0).astype(BF16))
    one_hot = jnp.concatenate(hits, axis=0)
    pool_loads[0].wait()
    w_load.start()
    goal_load.start()
    for load in pool_loads[1:]:
        load.wait()
    for piece in pieces:
        x_ref[:, piece] = jnp.dot(
            one_hot, pool_ref[:, piece], preferred_element_type=F32
        ).astype(BF16)
    w_load.wait()
    goal_load.wait()
    base = jnp.dot(x_ref[...], w_ref[...], preferred_element_type=F32) * inv_width

    overlaps = {}
    for s in range(0, STEPS - 1, 2):
        stop = min(s + 2, STEPS - 1)
        overlaps[s] = contract(
            x_ref[(s + 1) * batch :, :], x_ref[s * batch : stop * batch, :], ((1,), (1,))
        )

    spread = []
    for s in range(STEPS - 1):
        first = s // 2 * 2
        halves = []
        for t in range(s + 1, STEPS):
            down, across = (t - first - 1) * batch, (s - first) * batch
            block = overlaps[first][down : down + batch, across : across + batch]
            block = block * (reach(t - s) * inv_batch * inv_width)
            high = block.astype(BF16)
            halves += [high, (block - high.astype(F32)).astype(BF16)]
        spread.append(jnp.concatenate(halves, axis=0))

    hidden = [base[t * batch : (t + 1) * batch] for t in range(STEPS)]
    final = []
    for s in range(STEPS):
        sigma = jax.nn.sigmoid(hidden[s])
        wanted = goal_ref[s * batch : (s + 1) * batch, :].astype(F32)
        grad = (hidden[s] * sigma - wanted) * (sigma * (1.0 + hidden[s] * (1.0 - sigma)))
        if s < STEPS - 1:
            moved = jnp.dot(spread[s], grad.astype(BF16), preferred_element_type=F32)
            for n, t in enumerate(range(s + 1, STEPS)):
                at = 2 * n * batch
                hidden[t] = hidden[t] - (
                    moved[at : at + batch] + moved[at + batch : at + 2 * batch]
                )
        final.append((grad * (-reach(STEPS - s) * inv_batch)).T.astype(BF16))

    turned_ref[...] = jnp.concatenate(final, axis=1)
    share_rows(turned_ref, x_ref, partner, first_ref)
    start = pl.multiple_of(lax.axis_index("rep") * seg, seg)
    own_ref[...] = w_ref[pl.ds(start, seg), :]


def distances(parts):
    def far(distance):
        return (distance == 1, distance & 1, -(distance >> 1).bit_count(), distance)

    return [0, *sorted(range(1, parts), key=far)]


def pair_list(count):
    return [(i, j) for i in range(count) for j in range(i, count)]


def gram_kernel(order, known, *refs):
    count = len(order)
    deltas, before, out_ref = refs[:count], refs[count:-1], refs[-1]
    rows, seg = deltas[0].shape
    lanes = min(128, seg)
    block = min(8, count)
    tall = 16
    me = lax.axis_index("rep")
    down = lax.broadcasted_iota(jnp.int32, out_ref.shape, 0)
    across = lax.broadcasted_iota(jnp.int32, out_ref.shape, 1)
    table = before[0][...] if before else jnp.zeros(out_ref.shape, F32)
    for first in range(0, count, block):
        for second in range(first, count, block):
            pairs = [
                (i, j)
                for i in range(first, min(first + block, count))
                for j in range(second, min(second + block, count))
                if i <= j and j >= known
            ]
            if not pairs:
                continue
            members = sorted({k for pair in pairs for k in pair})

            def step(at, sums, pairs=pairs, members=members):
                sums = list(sums)
                row = pl.multiple_of(at * tall, tall)
                for lane in range(0, seg, lanes):
                    held = {
                        k: deltas[k][pl.ds(row, tall), lane : lane + lanes].astype(F32)
                        for k in members
                    }
                    for n, (i, j) in enumerate(pairs):
                        product = held[i] * held[j]
                        sums[n] = sums[n] + (product[:8] + product[8:])
                return tuple(sums)

            zeros = tuple(jnp.zeros((8, lanes), F32) for _ in pairs)
            sums = lax.fori_loop(0, rows // tall, step, zeros)
            for n, (i, j) in enumerate(pairs):
                value = jnp.sum(jnp.sum(sums[n], axis=0, keepdims=True), axis=1, keepdims=True)
                mine, other = me ^ order[i], me ^ order[j]
                spot = ((down == mine) & (across == other)) | ((down == other) & (across == mine))
                table = jnp.where(spot, value, table)
    out_ref[...] = table


def tree_weights(gram, count):
    weights = [None] * count
    current = dict(gram)
    width = 1
    while count > 1:
        left, right = [], []
        for i in range(0, count, 2):
            cross = current[i, i + 1]
            left_square = jnp.maximum(current[i, i], 0.0)
            right_square = jnp.maximum(current[i + 1, i + 1], 0.0)
            left.append(1.0 - cross / (2.0 * (left_square + EPSILON)))
            right.append(1.0 - cross / (2.0 * (right_square + EPSILON)))
        for i in range(count):
            scale = (right if i % 2 else left)[i // 2]
            for k in range(i * width, (i + 1) * width):
                weights[k] = scale if weights[k] is None else weights[k] * scale
        merged = {}
        for i in range(count // 2):
            for j in range(i, count // 2):

                def entry(a, b):
                    return current[min(a, b), max(a, b)]

                merged[i, j] = left[i] * (
                    left[j] * entry(2 * i, 2 * j) + right[j] * entry(2 * i, 2 * j + 1)
                ) + right[i] * (
                    left[j] * entry(2 * i + 1, 2 * j) + right[j] * entry(2 * i + 1, 2 * j + 1)
                )
        current = merged
        count //= 2
        width *= 2
    return weights


def combine_kernel(gram_ref, own_ref, *rest):
    deltas, out_ref = rest[:-1], rest[-1]
    count = len(deltas)
    me = lax.axis_index("rep")
    table = gram_ref[0]
    for member in range(1, gram_ref.shape[0]):
        table = table + gram_ref[member]
    gram = {(i, j): table[i : i + 1, j : j + 1] for i, j in pair_list(count)}
    weights = tree_weights(gram, count)
    total = None
    for distance, delta in zip(distances(count), deltas):
        weight = weights[0]
        for k in range(1, count):
            weight = jnp.where((me ^ distance) == k, weights[k], weight)
        term = weight * delta[...].astype(F32)
        total = term if total is None else total + term
    combined = total.T.astype(BF16).astype(F32)
    out_ref[...] = (own_ref[...].astype(F32) + combined).astype(BF16)


def place_kernel(*refs):
    pieces, (out_ref, sems) = refs[:-2], refs[-2:]
    seg = pieces[0].shape[0]
    me = lax.axis_index("rep")
    moves = []
    for distance, piece in enumerate(pieces):
        at = pl.multiple_of((me ^ distance) * seg, seg)
        move = pltpu.make_async_copy(piece, out_ref.at[pl.ds(at, seg)], sems.at[distance])
        move.start()
        moves.append(move)
    for move in moves:
        move.wait()


def call(kernel, out_shape, in_specs, scratch=(), out_specs=None):
    extra = {} if out_specs is None else {"out_specs": out_specs}
    return pl.pallas_call(
        kernel,
        out_shape=out_shape,
        in_specs=in_specs,
        scratch_shapes=scratch,
        compiler_params=pltpu.CompilerParams(vmem_limit_bytes=VMEM_LIMIT),
        **extra,
    )


def hold(value):
    return pltpu.with_memory_space_constraint(value, pltpu.HBM)


def flipped(value, replica_bits, shard_bits=0):
    replicas, shards = lax.axis_size("rep"), lax.axis_size("shard")
    pairs = [
        (i * shards + j, (i ^ replica_bits) * shards + (j ^ shard_bits))
        for i in range(replicas)
        for j in range(shards)
    ]
    return lax.ppermute(value, ("rep", "shard"), pairs)


def body(token_pool, row_index, weights, targets):
    parts = lax.axis_size("rep")
    width, columns = weights.shape[1:]
    cut = FF // columns
    seg = width // parts
    rows = row_index.shape[-1]
    pool_rows = token_pool.shape[1]
    near = pl.BlockSpec(memory_space=pltpu.VMEM)
    far = pl.BlockSpec(memory_space=pltpu.HBM)
    any_place = pl.BlockSpec(memory_space=pl.ANY)

    order = distances(parts)
    first = order[1]

    def local(*refs):
        local_kernel(cut, first, *refs)

    rows_out = jax.ShapeDtypeStruct((columns, seg), BF16)
    out, own_weights, turned, gathered = call(
        local,
        [
            rows_out,
            jax.ShapeDtypeStruct((seg, columns), BF16),
            jax.ShapeDtypeStruct((columns, rows), BF16),
            jax.ShapeDtypeStruct((rows, width), BF16),
        ],
        [far] * 4,
        [
            pltpu.VMEM((1, rows), jnp.int32),
            pltpu.VMEM((pool_rows, width), BF16),
            pltpu.VMEM((width, columns), BF16),
            pltpu.VMEM((rows, columns), BF16),
            pltpu.SemaphoreType.DMA((LOADS + 3,)),
        ],
    )(hold(row_index[0]), hold(token_pool[0]), hold(weights[0]), hold(targets[0, 0]))
    leaves = {first: flipped(out, first)}
    middle = max(2, parts - 3)
    for group, after in (
        ([0, *order[2:middle]], []),
        (order[middle:], [leaves[first]]),
    ):
        if not group:
            continue

        def shares(*refs, group=group):
            share_kernel(group, *refs)

        made = call(shares, [rows_out] * len(group), [near] * (2 + len(after)))(
            turned, gathered, *after
        )
        for d, out in zip(group, made):
            leaves[d] = flipped(out, d) if d else out

    tall = -(-parts // 8) * 8
    table = jax.ShapeDtypeStruct((tall, 128), F32)
    late = LATE if parts > LATE + 1 else 0
    soon = order[: parts - late]

    def first_gram(*refs):
        gram_kernel(soon, 0, *refs)

    def full_gram(*refs):
        gram_kernel(order, len(soon), *refs)

    gram = call(first_gram, table, [near] * len(soon))(*(leaves[d] for d in soon))
    if late:
        gram = call(full_gram, table, [near] * (parts + 1))(
            *(leaves[d] for d in order), gram
        )
    shards = lax.axis_size("shard")
    groups = [
        [i * shards + j for i in range(parts) for j in range(first, first + cut)]
        for first in range(0, shards, cut)
    ]
    groups = [group[::-1] for group in groups]
    gram = jnp.broadcast_to(gram, (parts * cut, *gram.shape))
    gram = lax.all_to_all(gram, ("rep", "shard"), 0, 0, axis_index_groups=groups)

    own = call(
        combine_kernel,
        jax.ShapeDtypeStruct((seg, columns), BF16),
        [near] * (parts + 2),
    )(gram, own_weights, *(leaves[d] for d in order))
    pieces = [own] + [None] * (parts - 1)
    pieces[1] = flipped(own, 1)
    for d in range(2, parts, 2):
        pieces[d + 1] = flipped(own, d + 1)
        pieces[d] = flipped(pieces[d + 1], 1)
    placed = call(
        place_kernel,
        jax.ShapeDtypeStruct((width, columns), BF16),
        [any_place] * parts,
        [pltpu.SemaphoreType.DMA((parts,))],
        far,
    )(*pieces)
    return placed[None]


def solution(mesh):
    in_specs = (
        P("rep", None, None),
        P("rep", None, None, None),
        P(None, None, "shard"),
        P("rep", None, None, "shard"),
    )
    out_specs = P(None, None, "shard")
    return jax.shard_map(body, mesh=mesh, in_specs=in_specs, out_specs=out_specs, check_vma=False)
```

```python
import math

import jax
import jax.numpy as jnp
from jax import lax
from jax.experimental import pallas as pl
from jax.experimental.pallas import tpu as pltpu
from jax.sharding import PartitionSpec as P

FF = 512
STEPS = 4
LEARN_RATE = 0.3
MOMENTUM = 0.9
EPSILON = 1e-06
LOADS = 4
LATE = 3
VMEM_LIMIT = 48 * 1024 * 1024

F32 = jnp.float32
BF16 = jnp.bfloat16


def reach(steps_between):
    return LEARN_RATE * sum(MOMENTUM**k for k in range(steps_between))


def contract(a, b, dims):
    return lax.dot_general(a, b, (dims, ((), ())), preferred_element_type=F32)


def share_rows(turned_ref, x_ref, distance, out_ref):
    seg = out_ref.shape[1]
    target = lax.axis_index("rep") ^ distance
    held = max(seg, 128)
    at = pl.multiple_of(target * seg // held * held, held)
    moved = jnp.dot(turned_ref[...], x_ref[:, pl.ds(at, held)], preferred_element_type=F32)
    share = moved[:, :seg]
    for place in range(1, held // seg):
        own = target % (held // seg) == place
        share = jnp.where(own, moved[:, place * seg : (place + 1) * seg], share)
    out_ref[...] = share.astype(BF16)


def share_kernel(order, turned_ref, x_ref, *rest):
    for distance, out_ref in zip(order, rest[-len(order) :]):
        share_rows(turned_ref, x_ref, distance, out_ref)


def local_kernel(cut, partner, idx_hbm, pool_hbm, w_hbm, goal_hbm, *rest):
    first_ref, own_ref, turned_ref, x_ref = rest[:4]
    idx_ref, pool_ref, w_ref, goal_ref, sems = rest[4:]
    pool_rows, width = pool_ref.shape
    seg = own_ref.shape[0]
    total_rows = idx_ref.shape[-1]
    batch = total_rows // STEPS
    inv_width = 1.0 / math.sqrt(width)
    inv_batch = 1.0 / math.sqrt(batch)
    share = width // LOADS
    pieces = [pl.ds(n * share, share) for n in range(LOADS)]

    idx_load = pltpu.make_async_copy(
        idx_hbm.at[lax.axis_index("shard") // cut], idx_ref, sems.at[len(pieces) + 2]
    )
    idx_load.start()
    pool_loads = []
    for n in range(LOADS):
        rows = pl.ds(n * (pool_rows // LOADS), pool_rows // LOADS)
        load = pltpu.make_async_copy(pool_hbm.at[rows], pool_ref.at[rows], sems.at[n])
        load.start()
        pool_loads.append(load)
    w_load = pltpu.make_async_copy(w_hbm, w_ref, sems.at[len(pieces)])
    goal_load = pltpu.make_async_copy(goal_hbm, goal_ref, sems.at[len(pieces) + 1])

    idx_load.wait()
    place = lax.broadcasted_iota(jnp.int32, (batch, pool_rows), 1)
    hits = []
    for t in range(STEPS):
        picked = jnp.broadcast_to(idx_ref[:, t * batch : (t + 1) * batch], (8, batch))
        picked = picked.astype(F32).T[:, :1].astype(jnp.int32)
        hits.append(jnp.where(place == picked, 1.0, 0.0).astype(BF16))
    one_hot = jnp.concatenate(hits, axis=0)
    pool_loads[0].wait()
    w_load.start()
    goal_load.start()
    for load in pool_loads[1:]:
        load.wait()
    for piece in pieces:
        x_ref[:, piece] = jnp.dot(
            one_hot, pool_ref[:, piece], preferred_element_type=F32
        ).astype(BF16)
    w_load.wait()
    goal_load.wait()
    base = jnp.dot(x_ref[...], w_ref[...], preferred_element_type=F32) * inv_width

    overlaps = {}
    for s in range(0, STEPS - 1, 2):
        stop = min(s + 2, STEPS - 1)
        overlaps[s] = contract(
            x_ref[(s + 1) * batch :, :], x_ref[s * batch : stop * batch, :], ((1,), (1,))
        )

    spread = []
    for s in range(STEPS - 1):
        first = s // 2 * 2
        halves = []
        for t in range(s + 1, STEPS):
            down, across = (t - first - 1) * batch, (s - first) * batch
            block = overlaps[first][down : down + batch, across : across + batch]
            block = block * (reach(t - s) * inv_batch * inv_width)
            high = block.astype(BF16)
            halves += [high, (block - high.astype(F32)).astype(BF16)]
        spread.append(jnp.concatenate(halves, axis=0))

    hidden = [base[t * batch : (t + 1) * batch] for t in range(STEPS)]
    final = []
    for s in range(STEPS):
        sigma = jax.nn.sigmoid(hidden[s])
        wanted = goal_ref[s * batch : (s + 1) * batch, :].astype(F32)
        grad = (hidden[s] * sigma - wanted) * (sigma * (1.0 + hidden[s] * (1.0 - sigma)))
        if s < STEPS - 1:
            moved = jnp.dot(spread[s], grad.astype(BF16), preferred_element_type=F32)
            for n, t in enumerate(range(s + 1, STEPS)):
                at = 2 * n * batch
                hidden[t] = hidden[t] - (
                    moved[at : at + batch] + moved[at + batch : at + 2 * batch]
                )
        final.append((grad * (-reach(STEPS - s) * inv_batch)).T.astype(BF16))

    turned_ref[...] = jnp.concatenate(final, axis=1)
    share_rows(turned_ref, x_ref, partner, first_ref)
    start = pl.multiple_of(lax.axis_index("rep") * seg, seg)
    own_ref[...] = w_ref[pl.ds(start, seg), :]


def distances(parts):
    def far(distance):
        return (distance == 1, distance & 1, -(distance >> 1).bit_count(), distance)

    return [0, *sorted(range(1, parts), key=far)]


def pair_list(count):
    return [(i, j) for i in range(count) for j in range(i, count)]


def gram_kernel(parts, order, known, *refs):
    count = len(order)
    deltas, before, out_ref = refs[:count], refs[count:-1], refs[-1]
    rows, seg = deltas[0].shape
    lanes = min(128, seg)
    block = min(8, count)
    tall = 16
    me = lax.axis_index("rep")
    down = lax.broadcasted_iota(jnp.int32, out_ref.shape, 0)
    spots = down * 128 + lax.broadcasted_iota(jnp.int32, out_ref.shape, 1)
    table = before[0][...] if before else jnp.zeros(out_ref.shape, F32)
    for first in range(0, count, block):
        for second in range(first, count, block):
            pairs = [
                (i, j)
                for i in range(first, min(first + block, count))
                for j in range(second, min(second + block, count))
                if i <= j and j >= known
            ]
            if not pairs:
                continue
            members = sorted({k for pair in pairs for k in pair})

            def step(at, sums, pairs=pairs, members=members):
                sums = list(sums)
                row = pl.multiple_of(at * tall, tall)
                for lane in range(0, seg, lanes):
                    held = {
                        k: deltas[k][pl.ds(row, tall), lane : lane + lanes].astype(F32)
                        for k in members
                    }
                    for n, (i, j) in enumerate(pairs):
                        product = held[i] * held[j]
                        sums[n] = sums[n] + (product[:8] + product[8:])
                return tuple(sums)

            zeros = tuple(jnp.zeros((8, lanes), F32) for _ in pairs)
            sums = lax.fori_loop(0, rows // tall, step, zeros, unroll=4 if count <= block else 1)
            for n, (i, j) in enumerate(pairs):
                value = jnp.sum(jnp.sum(sums[n], axis=0, keepdims=True), axis=1, keepdims=True)
                mine, other = me ^ order[i], me ^ order[j]
                here = (spots == mine * parts + other) | (spots == other * parts + mine)
                table = jnp.where(here, value, table)
    out_ref[...] = table


def tree_weights(gram, count):
    weights = [None] * count
    current = dict(gram)
    width = 1
    while count > 1:
        left, right = [], []
        for i in range(0, count, 2):
            cross = current[i, i + 1]
            left_square = jnp.maximum(current[i, i], 0.0)
            right_square = jnp.maximum(current[i + 1, i + 1], 0.0)
            left.append(1.0 - cross / (2.0 * (left_square + EPSILON)))
            right.append(1.0 - cross / (2.0 * (right_square + EPSILON)))
        for i in range(count):
            scale = (right if i % 2 else left)[i // 2]
            for k in range(i * width, (i + 1) * width):
                weights[k] = scale if weights[k] is None else weights[k] * scale
        merged = {}
        for i in range(count // 2):
            for j in range(i, count // 2):

                def entry(a, b):
                    return current[min(a, b), max(a, b)]

                merged[i, j] = left[i] * (
                    left[j] * entry(2 * i, 2 * j) + right[j] * entry(2 * i, 2 * j + 1)
                ) + right[i] * (
                    left[j] * entry(2 * i + 1, 2 * j) + right[j] * entry(2 * i + 1, 2 * j + 1)
                )
        current = merged
        count //= 2
        width *= 2
    return weights


def combine_kernel(gram_ref, own_ref, *rest):
    deltas, out_ref = rest[:-1], rest[-1]
    count = len(deltas)
    me = lax.axis_index("rep")
    table = gram_ref[0]
    for member in range(1, gram_ref.shape[0]):
        table = table + gram_ref[member]
    gram = {}
    for i, j in pair_list(count):
        down, across = divmod(i * count + j, 128)
        gram[i, j] = table[down : down + 1, across : across + 1]
    weights = tree_weights(gram, count)
    total = None
    for distance, delta in zip(distances(count), deltas):
        weight = weights[0]
        for k in range(1, count):
            weight = jnp.where((me ^ distance) == k, weights[k], weight)
        term = weight * delta[...].astype(F32)
        total = term if total is None else total + term
    combined = total.T.astype(BF16).astype(F32)
    out_ref[...] = (own_ref[...].astype(F32) + combined).astype(BF16)


def place_kernel(*refs):
    pieces, (out_ref, sems) = refs[:-2], refs[-2:]
    seg = pieces[0].shape[0]
    me = lax.axis_index("rep")
    moves = []
    for distance, piece in enumerate(pieces):
        at = pl.multiple_of((me ^ distance) * seg, seg)
        move = pltpu.make_async_copy(piece, out_ref.at[pl.ds(at, seg)], sems.at[distance])
        move.start()
        moves.append(move)
    for move in moves:
        move.wait()


def call(kernel, out_shape, in_specs, scratch=(), out_specs=None):
    extra = {} if out_specs is None else {"out_specs": out_specs}
    return pl.pallas_call(
        kernel,
        out_shape=out_shape,
        in_specs=in_specs,
        scratch_shapes=scratch,
        compiler_params=pltpu.CompilerParams(vmem_limit_bytes=VMEM_LIMIT),
        **extra,
    )


def hold(value):
    return pltpu.with_memory_space_constraint(value, pltpu.HBM)


def flipped(value, replica_bits, shard_bits=0):
    replicas, shards = lax.axis_size("rep"), lax.axis_size("shard")
    pairs = [
        (i * shards + j, (i ^ replica_bits) * shards + (j ^ shard_bits))
        for i in range(replicas)
        for j in range(shards)
    ]
    return lax.ppermute(value, ("rep", "shard"), pairs)


def body(token_pool, row_index, weights, targets):
    parts = lax.axis_size("rep")
    width, columns = weights.shape[1:]
    cut = FF // columns
    seg = width // parts
    rows = row_index.shape[-1]
    pool_rows = token_pool.shape[1]
    near = pl.BlockSpec(memory_space=pltpu.VMEM)
    far = pl.BlockSpec(memory_space=pltpu.HBM)
    any_place = pl.BlockSpec(memory_space=pl.ANY)

    order = distances(parts)
    first = order[1]

    def local(*refs):
        local_kernel(cut, first, *refs)

    rows_out = jax.ShapeDtypeStruct((columns, seg), BF16)
    out, own_weights, turned, gathered = call(
        local,
        [
            rows_out,
            jax.ShapeDtypeStruct((seg, columns), BF16),
            jax.ShapeDtypeStruct((columns, rows), BF16),
            jax.ShapeDtypeStruct((rows, width), BF16),
        ],
        [far] * 4,
        [
            pltpu.VMEM((1, rows), jnp.int32),
            pltpu.VMEM((pool_rows, width), BF16),
            pltpu.VMEM((width, columns), BF16),
            pltpu.VMEM((rows, columns), BF16),
            pltpu.SemaphoreType.DMA((LOADS + 3,)),
        ],
    )(hold(row_index[0]), hold(token_pool[0]), hold(weights[0]), hold(targets[0, 0]))
    leaves = {first: flipped(out, first)}
    middle = max(2, parts - 2)
    for group, after in (
        ([0, *order[2:middle]], []),
        (order[middle:], [leaves[first]]),
    ):
        if not group:
            continue

        def shares(*refs, group=group):
            share_kernel(group, *refs)

        made = call(shares, [rows_out] * len(group), [near] * (2 + len(after)))(
            turned, gathered, *after
        )
        for d, out in zip(group, made):
            leaves[d] = flipped(out, d) if d else out

    table = jax.ShapeDtypeStruct((-(-parts * parts // 128), 128), F32)
    gram, known = [], 0
    for reached in (parts - 3, parts - 2, parts):
        if reached <= known:
            continue
        taken = order[:reached]

        def products(*refs, taken=taken, known=known):
            gram_kernel(parts, taken, known, *refs)

        inputs = [leaves[d] for d in taken] + gram
        gram, known = [call(products, table, [near] * len(inputs))(*inputs)], reached
    gram = gram[0]
    shards = lax.axis_size("shard")
    groups = [
        [i * shards + j for i in range(parts) for j in range(first, first + cut)]
        for first in range(0, shards, cut)
    ]
    groups = [group[::-1] for group in groups]
    gram = jnp.broadcast_to(gram, (parts * cut, *gram.shape))
    gram = lax.all_to_all(gram, ("rep", "shard"), 0, 0, axis_index_groups=groups)

    own = call(
        combine_kernel,
        jax.ShapeDtypeStruct((seg, columns), BF16),
        [near] * (parts + 2),
    )(gram, own_weights, *(leaves[d] for d in order))
    pieces = [own] + [None] * (parts - 1)
    pieces[1] = flipped(own, 1)
    for d in range(2, parts, 2):
        pieces[d + 1] = flipped(own, d + 1)
        pieces[d] = flipped(pieces[d + 1], 1)
    placed = call(
        place_kernel,
        jax.ShapeDtypeStruct((width, columns), BF16),
        [any_place] * parts,
        [pltpu.SemaphoreType.DMA((parts,))],
        far,
    )(*pieces)
    return placed[None]


def solution(mesh):
    in_specs = (
        P("rep", None, None),
        P("rep", None, None, None),
        P(None, None, "shard"),
        P("rep", None, None, "shard"),
    )
    out_specs = P(None, None, "shard")
    return jax.shard_map(body, mesh=mesh, in_specs=in_specs, out_specs=out_specs, check_vma=False)
```

```python
import math

import jax
import jax.numpy as jnp
from jax import lax
from jax.experimental import pallas as pl
from jax.experimental.pallas import tpu as pltpu
from jax.sharding import PartitionSpec as P

FF = 512
STEPS = 4
LEARN_RATE = 0.3
MOMENTUM = 0.9
EPSILON = 1e-06
LOADS = 4
VMEM_LIMIT = 48 * 1024 * 1024

F32 = jnp.float32
BF16 = jnp.bfloat16


def reach(steps_between):
    return LEARN_RATE * sum(MOMENTUM**k for k in range(steps_between))


def contract(a, b, dims):
    return lax.dot_general(a, b, (dims, ((), ())), preferred_element_type=F32)


def share_rows(turned_ref, x_ref, distance, out_ref):
    seg = out_ref.shape[1]
    target = lax.axis_index("rep") ^ distance
    held = max(seg, 128)
    at = pl.multiple_of(target * seg // held * held, held)
    moved = jnp.dot(turned_ref[...], x_ref[:, pl.ds(at, held)], preferred_element_type=F32)
    share = moved[:, :seg]
    for place in range(1, held // seg):
        own = target % (held // seg) == place
        share = jnp.where(own, moved[:, place * seg : (place + 1) * seg], share)
    out_ref[...] = share.astype(BF16)


def share_kernel(order, turned_ref, x_ref, *rest):
    for distance, out_ref in zip(order, rest[-len(order) :]):
        share_rows(turned_ref, x_ref, distance, out_ref)


def local_kernel(cut, partner, idx_hbm, pool_hbm, w_hbm, goal_hbm, *rest):
    first_ref, own_ref, turned_ref, x_ref = rest[:4]
    idx_ref, pool_ref, w_ref, goal_ref, sems = rest[4:]
    pool_rows, width = pool_ref.shape
    seg = own_ref.shape[0]
    total_rows = idx_ref.shape[-1]
    batch = total_rows // STEPS
    inv_width = 1.0 / math.sqrt(width)
    inv_batch = 1.0 / math.sqrt(batch)
    share = width // LOADS
    pieces = [pl.ds(n * share, share) for n in range(LOADS)]

    idx_load = pltpu.make_async_copy(
        idx_hbm.at[lax.axis_index("shard") // cut], idx_ref, sems.at[len(pieces) + 2]
    )
    idx_load.start()
    pool_loads = []
    for n in range(LOADS):
        rows = pl.ds(n * (pool_rows // LOADS), pool_rows // LOADS)
        load = pltpu.make_async_copy(pool_hbm.at[rows], pool_ref.at[rows], sems.at[n])
        load.start()
        pool_loads.append(load)
    w_load = pltpu.make_async_copy(w_hbm, w_ref, sems.at[len(pieces)])
    goal_load = pltpu.make_async_copy(goal_hbm, goal_ref, sems.at[len(pieces) + 1])

    idx_load.wait()
    place = lax.broadcasted_iota(jnp.int32, (batch, pool_rows), 1)
    hits = []
    for t in range(STEPS):
        picked = jnp.broadcast_to(idx_ref[:, t * batch : (t + 1) * batch], (8, batch))
        picked = picked.astype(F32).T[:, :1].astype(jnp.int32)
        hits.append(jnp.where(place == picked, 1.0, 0.0).astype(BF16))
    one_hot = jnp.concatenate(hits, axis=0)
    pool_loads[0].wait()
    w_load.start()
    goal_load.start()
    for load in pool_loads[1:]:
        load.wait()
    for piece in pieces:
        x_ref[:, piece] = jnp.dot(
            one_hot, pool_ref[:, piece], preferred_element_type=F32
        ).astype(BF16)
    w_load.wait()
    goal_load.wait()
    base = jnp.dot(x_ref[...], w_ref[...], preferred_element_type=F32) * inv_width

    overlaps = {}
    for s in range(0, STEPS - 1, 2):
        stop = min(s + 2, STEPS - 1)
        overlaps[s] = contract(
            x_ref[(s + 1) * batch :, :], x_ref[s * batch : stop * batch, :], ((1,), (1,))
        )

    spread = []
    for s in range(STEPS - 1):
        first = s // 2 * 2
        halves = []
        for t in range(s + 1, STEPS):
            down, across = (t - first - 1) * batch, (s - first) * batch
            block = overlaps[first][down : down + batch, across : across + batch]
            block = block * (reach(t - s) * inv_batch * inv_width)
            high = block.astype(BF16)
            halves += [high, (block - high.astype(F32)).astype(BF16)]
        spread.append(jnp.concatenate(halves, axis=0))

    hidden = [base[t * batch : (t + 1) * batch] for t in range(STEPS)]
    final = []
    for s in range(STEPS):
        sigma = jax.nn.sigmoid(hidden[s])
        wanted = goal_ref[s * batch : (s + 1) * batch, :].astype(F32)
        grad = (hidden[s] * sigma - wanted) * (sigma * (1.0 + hidden[s] * (1.0 - sigma)))
        if s < STEPS - 1:
            moved = jnp.dot(spread[s], grad.astype(BF16), preferred_element_type=F32)
            for n, t in enumerate(range(s + 1, STEPS)):
                at = 2 * n * batch
                hidden[t] = hidden[t] - (
                    moved[at : at + batch] + moved[at + batch : at + 2 * batch]
                )
        final.append((grad * (-reach(STEPS - s) * inv_batch)).T.astype(BF16))

    turned_ref[...] = jnp.concatenate(final, axis=1)
    share_rows(turned_ref, x_ref, partner, first_ref)
    start = pl.multiple_of(lax.axis_index("rep") * seg, seg)
    own_ref[...] = w_ref[pl.ds(start, seg), :]


def distances(parts):
    def far(distance):
        return (distance == 1, distance & 1, -(distance >> 1).bit_count(), distance)

    return [0, *sorted(range(1, parts), key=far)]


def pair_list(count):
    return [(i, j) for i in range(count) for j in range(i, count)]


def gram_kernel(parts, order, known, *refs):
    count = len(order)
    deltas, before, out_ref = refs[:count], refs[count:-1], refs[-1]
    rows, seg = deltas[0].shape
    lanes = min(128, seg)
    block = min(8, count)
    tall = 16
    me = lax.axis_index("rep")
    down = lax.broadcasted_iota(jnp.int32, out_ref.shape, 0)
    spots = down * 128 + lax.broadcasted_iota(jnp.int32, out_ref.shape, 1)
    table = before[0][...] if before else jnp.zeros(out_ref.shape, F32)
    for first in range(0, count, block):
        for second in range(first, count, block):
            pairs = [
                (i, j)
                for i in range(first, min(first + block, count))
                for j in range(second, min(second + block, count))
                if i <= j and j >= known
            ]
            if not pairs:
                continue
            members = sorted({k for pair in pairs for k in pair})

            def step(at, sums, pairs=pairs, members=members):
                sums = list(sums)
                row = pl.multiple_of(at * tall, tall)
                for lane in range(0, seg, lanes):
                    held = {
                        k: deltas[k][pl.ds(row, tall), lane : lane + lanes].astype(F32)
                        for k in members
                    }
                    for n, (i, j) in enumerate(pairs):
                        product = held[i] * held[j]
                        sums[n] = sums[n] + (product[:8] + product[8:])
                return tuple(sums)

            zeros = tuple(jnp.zeros((8, lanes), F32) for _ in pairs)
            sums = lax.fori_loop(0, rows // tall, step, zeros, unroll=4 if count <= block else 1)
            for n, (i, j) in enumerate(pairs):
                value = jnp.sum(jnp.sum(sums[n], axis=0, keepdims=True), axis=1, keepdims=True)
                mine, other = me ^ order[i], me ^ order[j]
                here = (spots == mine * parts + other) | (spots == other * parts + mine)
                table = jnp.where(here, value, table)
    out_ref[...] = table


def tree_weights(gram, count):
    weights = [None] * count
    current = dict(gram)
    width = 1
    while count > 1:
        left, right = [], []
        for i in range(0, count, 2):
            cross = current[i, i + 1]
            left_square = jnp.maximum(current[i, i], 0.0)
            right_square = jnp.maximum(current[i + 1, i + 1], 0.0)
            left.append(1.0 - cross / (2.0 * (left_square + EPSILON)))
            right.append(1.0 - cross / (2.0 * (right_square + EPSILON)))
        for i in range(count):
            scale = (right if i % 2 else left)[i // 2]
            for k in range(i * width, (i + 1) * width):
                weights[k] = scale if weights[k] is None else weights[k] * scale
        merged = {}
        for i in range(count // 2):
            for j in range(i, count // 2):

                def entry(a, b):
                    return current[min(a, b), max(a, b)]

                merged[i, j] = left[i] * (
                    left[j] * entry(2 * i, 2 * j) + right[j] * entry(2 * i, 2 * j + 1)
                ) + right[i] * (
                    left[j] * entry(2 * i + 1, 2 * j) + right[j] * entry(2 * i + 1, 2 * j + 1)
                )
        current = merged
        count //= 2
        width *= 2
    return weights


def combine_kernel(gram_ref, own_ref, *rest):
    deltas, out_ref = rest[:-1], rest[-1]
    count = len(deltas)
    me = lax.axis_index("rep")
    table = gram_ref[0]
    for member in range(1, gram_ref.shape[0]):
        table = table + gram_ref[member]
    gram = {}
    for i, j in pair_list(count):
        down, across = divmod(i * count + j, 128)
        gram[i, j] = table[down : down + 1, across : across + 1]
    weights = tree_weights(gram, count)
    total = None
    for distance, delta in zip(distances(count), deltas):
        weight = weights[0]
        for k in range(1, count):
            weight = jnp.where((me ^ distance) == k, weights[k], weight)
        term = weight * delta[...].astype(F32)
        total = term if total is None else total + term
    combined = total.T.astype(BF16).astype(F32)
    out_ref[...] = (own_ref[...].astype(F32) + combined).astype(BF16)


def place_kernel(routes, *refs):
    pieces, (out_ref, sems) = refs[:-2], refs[-2:]
    seg = pieces[0].shape[0]
    me = lax.axis_index("rep")
    moves = []
    for n, ((even, odd), piece) in enumerate(zip(routes, pieces)):
        distance = jnp.where(me % 2 == 1, odd, even)
        at = pl.multiple_of((me ^ distance) * seg, seg)
        move = pltpu.make_async_copy(piece, out_ref.at[pl.ds(at, seg)], sems.at[n])
        move.start()
        moves.append(move)
    for move in moves:
        move.wait()


def call(kernel, out_shape, in_specs, scratch=(), out_specs=None):
    extra = {} if out_specs is None else {"out_specs": out_specs}
    return pl.pallas_call(
        kernel,
        out_shape=out_shape,
        in_specs=in_specs,
        scratch_shapes=scratch,
        compiler_params=pltpu.CompilerParams(vmem_limit_bytes=VMEM_LIMIT),
        **extra,
    )


def hold(value):
    return pltpu.with_memory_space_constraint(value, pltpu.HBM)


def flipped(value, replica_bits, shard_bits=0):
    replicas, shards = lax.axis_size("rep"), lax.axis_size("shard")
    bits = replica_bits if isinstance(replica_bits, tuple) else (replica_bits,) * 2
    pairs = [
        (i * shards + j, (i ^ bits[i % 2]) * shards + (j ^ shard_bits))
        for i in range(replicas)
        for j in range(shards)
    ]
    return lax.ppermute(value, ("rep", "shard"), pairs)


def body(token_pool, row_index, weights, targets):
    parts = lax.axis_size("rep")
    width, columns = weights.shape[1:]
    cut = FF // columns
    seg = width // parts
    rows = row_index.shape[-1]
    pool_rows = token_pool.shape[1]
    near = pl.BlockSpec(memory_space=pltpu.VMEM)
    far = pl.BlockSpec(memory_space=pltpu.HBM)
    any_place = pl.BlockSpec(memory_space=pl.ANY)

    order = distances(parts)
    first = order[1]

    def local(*refs):
        local_kernel(cut, first, *refs)

    rows_out = jax.ShapeDtypeStruct((columns, seg), BF16)
    out, own_weights, turned, gathered = call(
        local,
        [
            rows_out,
            jax.ShapeDtypeStruct((seg, columns), BF16),
            jax.ShapeDtypeStruct((columns, rows), BF16),
            jax.ShapeDtypeStruct((rows, width), BF16),
        ],
        [far] * 4,
        [
            pltpu.VMEM((1, rows), jnp.int32),
            pltpu.VMEM((pool_rows, width), BF16),
            pltpu.VMEM((width, columns), BF16),
            pltpu.VMEM((rows, columns), BF16),
            pltpu.SemaphoreType.DMA((LOADS + 3,)),
        ],
    )(hold(row_index[0]), hold(token_pool[0]), hold(weights[0]), hold(targets[0, 0]))
    leaves = {first: flipped(out, first)}
    middle = max(2, parts - 2)
    for group, after in (
        ([0, *order[2:middle]], []),
        (order[middle:], [leaves[first]]),
    ):
        if not group:
            continue

        def shares(*refs, group=group):
            share_kernel(group, *refs)

        made = call(shares, [rows_out] * len(group), [near] * (2 + len(after)))(
            turned, gathered, *after
        )
        for d, out in zip(group, made):
            leaves[d] = flipped(out, d) if d else out

    table = jax.ShapeDtypeStruct((-(-parts * parts // 128), 128), F32)
    gram, known = [], 0
    for reached in (parts - 3, parts - 2, parts):
        if reached <= known:
            continue
        taken = order[:reached]

        def products(*refs, taken=taken, known=known):
            gram_kernel(parts, taken, known, *refs)

        inputs = [leaves[d] for d in taken] + gram
        gram, known = [call(products, table, [near] * len(inputs))(*inputs)], reached
    gram = gram[0]
    shards = lax.axis_size("shard")
    groups = [
        [i * shards + j for i in range(parts) for j in range(first, first + cut)]
        for first in range(0, shards, cut)
    ]
    groups = [group[::-1] for group in groups]
    gram = jnp.broadcast_to(gram, (parts * cut, *gram.shape))
    gram = lax.all_to_all(gram, ("rep", "shard"), 0, 0, axis_index_groups=groups)

    own = call(
        combine_kernel,
        jax.ShapeDtypeStruct((seg, columns), BF16),
        [near] * (parts + 2),
    )(gram, own_weights, *(leaves[d] for d in order))
    pieces = {(0, 0): own, (1, 1): flipped(own, 1)}
    bits = parts.bit_length() - 2
    for chip in range(parts // 2 - 1, 0, -1):
        mirror = sum((chip >> k & 1) << (bits - 1 - k) for k in range(bits))
        if mirror == chip:
            came, passed = (2 * chip + 1, 2 * chip + 1), (2 * chip, 2 * chip)
        else:
            came, passed = (2 * chip, 2 * mirror), (2 * mirror + 1, 2 * chip + 1)
        pieces[came] = flipped(own, came)
        pieces[passed] = flipped(pieces[came], 1)

    def place(*refs):
        place_kernel(list(pieces), *refs)

    placed = call(
        place,
        jax.ShapeDtypeStruct((width, columns), BF16),
        [any_place] * parts,
        [pltpu.SemaphoreType.DMA((parts,))],
        far,
    )(*pieces.values())
    return placed[None]


def solution(mesh):
    in_specs = (
        P("rep", None, None),
        P("rep", None, None, None),
        P(None, None, "shard"),
        P("rep", None, None, "shard"),
    )
    out_specs = P(None, None, "shard")
    return jax.shard_map(body, mesh=mesh, in_specs=in_specs, out_specs=out_specs, check_vma=False)
```

```python
import math

import jax
import jax.numpy as jnp
from jax import lax
from jax.experimental import pallas as pl
from jax.experimental.pallas import tpu as pltpu
from jax.sharding import PartitionSpec as P

FF = 512
STEPS = 4
LEARN_RATE = 0.3
MOMENTUM = 0.9
EPSILON = 1e-06
LOADS = 4
VMEM_LIMIT = 48 * 1024 * 1024

F32 = jnp.float32
BF16 = jnp.bfloat16


def reach(steps_between):
    return LEARN_RATE * sum(MOMENTUM**k for k in range(steps_between))


def contract(a, b, dims):
    return lax.dot_general(a, b, (dims, ((), ())), preferred_element_type=F32)


def routes(parts):
    bits = parts.bit_length() - 2
    ways = {}
    for distance in range(parts):
        chip = distance >> 1
        mirror = sum((chip >> k & 1) << (bits - 1 - k) for k in range(bits))
        ways[distance] = (distance, distance if distance & 1 else 2 * mirror)
    return ways


def partner(me, way):
    return me ^ jnp.where(me % 2 == 1, way[1], way[0])


def share_rows(turned_ref, x_ref, way, out_ref):
    seg = out_ref.shape[1]
    target = partner(lax.axis_index("rep"), way)
    held = max(seg, 128)
    at = pl.multiple_of(target * seg // held * held, held)
    moved = jnp.dot(turned_ref[...], x_ref[:, pl.ds(at, held)], preferred_element_type=F32)
    share = moved[:, :seg]
    for place in range(1, held // seg):
        own = target % (held // seg) == place
        share = jnp.where(own, moved[:, place * seg : (place + 1) * seg], share)
    out_ref[...] = share.astype(BF16)


def share_kernel(order, turned_ref, x_ref, *rest):
    for way, out_ref in zip(order, rest[-len(order) :]):
        share_rows(turned_ref, x_ref, way, out_ref)


def local_kernel(cut, way, idx_hbm, pool_hbm, w_hbm, goal_hbm, *rest):
    first_ref, own_ref, turned_ref, x_ref = rest[:4]
    idx_ref, pool_ref, w_ref, goal_ref, sems = rest[4:]
    pool_rows, width = pool_ref.shape
    seg = own_ref.shape[0]
    total_rows = idx_ref.shape[-1]
    batch = total_rows // STEPS
    inv_width = 1.0 / math.sqrt(width)
    inv_batch = 1.0 / math.sqrt(batch)
    share = width // LOADS
    pieces = [pl.ds(n * share, share) for n in range(LOADS)]

    idx_load = pltpu.make_async_copy(
        idx_hbm.at[lax.axis_index("shard") // cut], idx_ref, sems.at[len(pieces) + 2]
    )
    idx_load.start()
    pool_loads = []
    for n in range(LOADS):
        rows = pl.ds(n * (pool_rows // LOADS), pool_rows // LOADS)
        load = pltpu.make_async_copy(pool_hbm.at[rows], pool_ref.at[rows], sems.at[n])
        load.start()
        pool_loads.append(load)
    w_load = pltpu.make_async_copy(w_hbm, w_ref, sems.at[len(pieces)])
    goal_load = pltpu.make_async_copy(goal_hbm, goal_ref, sems.at[len(pieces) + 1])

    idx_load.wait()
    place = lax.broadcasted_iota(jnp.int32, (batch, pool_rows), 1)
    hits = []
    for t in range(STEPS):
        picked = jnp.broadcast_to(idx_ref[:, t * batch : (t + 1) * batch], (8, batch))
        picked = picked.astype(F32).T[:, :1].astype(jnp.int32)
        hits.append(jnp.where(place == picked, 1.0, 0.0).astype(BF16))
    one_hot = jnp.concatenate(hits, axis=0)
    pool_loads[0].wait()
    w_load.start()
    goal_load.start()
    for load in pool_loads[1:]:
        load.wait()
    for piece in pieces:
        x_ref[:, piece] = jnp.dot(
            one_hot, pool_ref[:, piece], preferred_element_type=F32
        ).astype(BF16)
    w_load.wait()
    goal_load.wait()
    base = jnp.dot(x_ref[...], w_ref[...], preferred_element_type=F32) * inv_width

    overlaps = {}
    for s in range(0, STEPS - 1, 2):
        stop = min(s + 2, STEPS - 1)
        overlaps[s] = contract(
            x_ref[(s + 1) * batch :, :], x_ref[s * batch : stop * batch, :], ((1,), (1,))
        )

    spread = []
    for s in range(STEPS - 1):
        first = s // 2 * 2
        halves = []
        for t in range(s + 1, STEPS):
            down, across = (t - first - 1) * batch, (s - first) * batch
            block = overlaps[first][down : down + batch, across : across + batch]
            block = block * (reach(t - s) * inv_batch * inv_width)
            high = block.astype(BF16)
            halves += [high, (block - high.astype(F32)).astype(BF16)]
        spread.append(jnp.concatenate(halves, axis=0))

    hidden = [base[t * batch : (t + 1) * batch] for t in range(STEPS)]
    final = []
    for s in range(STEPS):
        sigma = jax.nn.sigmoid(hidden[s])
        wanted = goal_ref[s * batch : (s + 1) * batch, :].astype(F32)
        grad = (hidden[s] * sigma - wanted) * (sigma * (1.0 + hidden[s] * (1.0 - sigma)))
        if s < STEPS - 1:
            moved = jnp.dot(spread[s], grad.astype(BF16), preferred_element_type=F32)
            for n, t in enumerate(range(s + 1, STEPS)):
                at = 2 * n * batch
                hidden[t] = hidden[t] - (
                    moved[at : at + batch] + moved[at + batch : at + 2 * batch]
                )
        final.append((grad * (-reach(STEPS - s) * inv_batch)).T.astype(BF16))

    turned_ref[...] = jnp.concatenate(final, axis=1)
    share_rows(turned_ref, x_ref, way, first_ref)
    start = pl.multiple_of(lax.axis_index("rep") * seg, seg)
    own_ref[...] = w_ref[pl.ds(start, seg), :]


def distances(parts):
    def far(distance):
        return (distance == 1, distance & 1, -(distance >> 1).bit_count(), distance)

    return [0, *sorted(range(1, parts), key=far)]


def pair_list(count):
    return [(i, j) for i in range(count) for j in range(i, count)]


def gram_kernel(parts, order, known, *refs):
    count = len(order)
    deltas, before, out_ref = refs[:count], refs[count:-1], refs[-1]
    rows, seg = deltas[0].shape
    lanes = min(128, seg)
    block = min(8, count)
    tall = 16
    me = lax.axis_index("rep")
    down = lax.broadcasted_iota(jnp.int32, out_ref.shape, 0)
    spots = down * 128 + lax.broadcasted_iota(jnp.int32, out_ref.shape, 1)
    table = before[0][...] if before else jnp.zeros(out_ref.shape, F32)
    for first in range(0, count, block):
        for second in range(first, count, block):
            pairs = [
                (i, j)
                for i in range(first, min(first + block, count))
                for j in range(second, min(second + block, count))
                if i <= j and j >= known
            ]
            if not pairs:
                continue
            members = sorted({k for pair in pairs for k in pair})

            def step(at, sums, pairs=pairs, members=members):
                sums = list(sums)
                row = pl.multiple_of(at * tall, tall)
                for lane in range(0, seg, lanes):
                    held = {
                        k: deltas[k][pl.ds(row, tall), lane : lane + lanes].astype(F32)
                        for k in members
                    }
                    for n, (i, j) in enumerate(pairs):
                        product = held[i] * held[j]
                        sums[n] = sums[n] + (product[:8] + product[8:])
                return tuple(sums)

            zeros = tuple(jnp.zeros((8, lanes), F32) for _ in pairs)
            sums = lax.fori_loop(0, rows // tall, step, zeros, unroll=4 if count <= block else 1)
            for n, (i, j) in enumerate(pairs):
                value = jnp.sum(jnp.sum(sums[n], axis=0, keepdims=True), axis=1, keepdims=True)
                mine, other = partner(me, order[i]), partner(me, order[j])
                here = (spots == mine * parts + other) | (spots == other * parts + mine)
                table = jnp.where(here, value, table)
    out_ref[...] = table


def tree_weights(gram, count):
    weights = [None] * count
    current = dict(gram)
    width = 1
    while count > 1:
        left, right = [], []
        for i in range(0, count, 2):
            cross = current[i, i + 1]
            left_square = jnp.maximum(current[i, i], 0.0)
            right_square = jnp.maximum(current[i + 1, i + 1], 0.0)
            left.append(1.0 - cross / (2.0 * (left_square + EPSILON)))
            right.append(1.0 - cross / (2.0 * (right_square + EPSILON)))
        for i in range(count):
            scale = (right if i % 2 else left)[i // 2]
            for k in range(i * width, (i + 1) * width):
                weights[k] = scale if weights[k] is None else weights[k] * scale
        merged = {}
        for i in range(count // 2):
            for j in range(i, count // 2):

                def entry(a, b):
                    return current[min(a, b), max(a, b)]

                merged[i, j] = left[i] * (
                    left[j] * entry(2 * i, 2 * j) + right[j] * entry(2 * i, 2 * j + 1)
                ) + right[i] * (
                    left[j] * entry(2 * i + 1, 2 * j) + right[j] * entry(2 * i + 1, 2 * j + 1)
                )
        current = merged
        count //= 2
        width *= 2
    return weights


def combine_kernel(gram_ref, own_ref, *rest):
    deltas, out_ref = rest[:-1], rest[-1]
    count = len(deltas)
    me = lax.axis_index("rep")
    table = gram_ref[0]
    for member in range(1, gram_ref.shape[0]):
        table = table + gram_ref[member]
    gram = {}
    for i, j in pair_list(count):
        down, across = divmod(i * count + j, 128)
        gram[i, j] = table[down : down + 1, across : across + 1]
    weights = tree_weights(gram, count)
    total = None
    ways = routes(count)
    for distance, delta in zip(distances(count), deltas):
        weight = weights[0]
        for k in range(1, count):
            weight = jnp.where(partner(me, ways[distance]) == k, weights[k], weight)
        term = weight * delta[...].astype(F32)
        total = term if total is None else total + term
    combined = total.T.astype(BF16).astype(F32)
    out_ref[...] = (own_ref[...].astype(F32) + combined).astype(BF16)


def place_kernel(ways, *refs):
    pieces, (out_ref, sems) = refs[:-2], refs[-2:]
    seg = pieces[0].shape[0]
    me = lax.axis_index("rep")
    moves = []
    for n, (way, piece) in enumerate(zip(ways, pieces)):
        at = pl.multiple_of(partner(me, way) * seg, seg)
        move = pltpu.make_async_copy(piece, out_ref.at[pl.ds(at, seg)], sems.at[n])
        move.start()
        moves.append(move)
    for move in moves:
        move.wait()


def call(kernel, out_shape, in_specs, scratch=(), out_specs=None):
    extra = {} if out_specs is None else {"out_specs": out_specs}
    return pl.pallas_call(
        kernel,
        out_shape=out_shape,
        in_specs=in_specs,
        scratch_shapes=scratch,
        compiler_params=pltpu.CompilerParams(vmem_limit_bytes=VMEM_LIMIT),
        **extra,
    )


def hold(value):
    return pltpu.with_memory_space_constraint(value, pltpu.HBM)


def flipped(value, way, shard_bits=0):
    replicas, shards = lax.axis_size("rep"), lax.axis_size("shard")
    bits = way if isinstance(way, tuple) else (way, way)
    pairs = [
        (i * shards + j, (i ^ bits[i % 2]) * shards + (j ^ shard_bits))
        for i in range(replicas)
        for j in range(shards)
    ]
    return lax.ppermute(value, ("rep", "shard"), pairs)


def body(token_pool, row_index, weights, targets):
    parts = lax.axis_size("rep")
    width, columns = weights.shape[1:]
    cut = FF // columns
    seg = width // parts
    rows = row_index.shape[-1]
    pool_rows = token_pool.shape[1]
    near = pl.BlockSpec(memory_space=pltpu.VMEM)
    far = pl.BlockSpec(memory_space=pltpu.HBM)
    any_place = pl.BlockSpec(memory_space=pl.ANY)

    order, ways = distances(parts), routes(parts)
    first = order[1]

    def local(*refs):
        local_kernel(cut, ways[first], *refs)

    rows_out = jax.ShapeDtypeStruct((columns, seg), BF16)
    out, own_weights, turned, gathered = call(
        local,
        [
            rows_out,
            jax.ShapeDtypeStruct((seg, columns), BF16),
            jax.ShapeDtypeStruct((columns, rows), BF16),
            jax.ShapeDtypeStruct((rows, width), BF16),
        ],
        [far] * 4,
        [
            pltpu.VMEM((1, rows), jnp.int32),
            pltpu.VMEM((pool_rows, width), BF16),
            pltpu.VMEM((width, columns), BF16),
            pltpu.VMEM((rows, columns), BF16),
            pltpu.SemaphoreType.DMA((LOADS + 3,)),
        ],
    )(hold(row_index[0]), hold(token_pool[0]), hold(weights[0]), hold(targets[0, 0]))
    leaves = {first: flipped(out, ways[first])}
    middle = max(2, parts - 2)
    for group, after in (
        ([0, *order[2:middle]], []),
        (order[middle:], [leaves[first]]),
    ):
        if not group:
            continue

        def shares(*refs, group=group):
            share_kernel([ways[d] for d in group], *refs)

        made = call(shares, [rows_out] * len(group), [near] * (2 + len(after)))(
            turned, gathered, *after
        )
        for d, out in zip(group, made):
            leaves[d] = flipped(out, ways[d]) if d else out

    table = jax.ShapeDtypeStruct((-(-parts * parts // 128), 128), F32)
    gram, known = [], 0
    for reached in (parts - 3, parts - 2, parts):
        if reached <= known:
            continue
        taken = order[:reached]

        def products(*refs, taken=taken, known=known):
            gram_kernel(parts, [ways[d] for d in taken], known, *refs)

        inputs = [leaves[d] for d in taken] + gram
        gram, known = [call(products, table, [near] * len(inputs))(*inputs)], reached
    gram = gram[0]
    shards = lax.axis_size("shard")
    groups = [
        [i * shards + j for i in range(parts) for j in range(first, first + cut)]
        for first in range(0, shards, cut)
    ]
    groups = [group[::-1] for group in groups]
    gram = jnp.broadcast_to(gram, (parts * cut, *gram.shape))
    gram = lax.all_to_all(gram, ("rep", "shard"), 0, 0, axis_index_groups=groups)

    own = call(
        combine_kernel,
        jax.ShapeDtypeStruct((seg, columns), BF16),
        [near] * (parts + 2),
    )(gram, own_weights, *(leaves[d] for d in order))
    pieces = {ways[0]: own, ways[1]: flipped(own, 1)}
    chips = sorted(range(1, parts // 2), key=lambda chip: (chip & 1, -chip))
    for chip in [*(c for c in chips if c != 1), 1]:
        came = ways[2 * chip]
        if came[0] == came[1]:
            came = ways[2 * chip + 1]
        passed = (came[1] ^ 1, came[0] ^ 1)
        pieces[came] = flipped(own, came)
        pieces[passed] = flipped(pieces[came], 1)

    def place(*refs):
        place_kernel(list(pieces), *refs)

    placed = call(
        place,
        jax.ShapeDtypeStruct((width, columns), BF16),
        [any_place] * parts,
        [pltpu.SemaphoreType.DMA((parts,))],
        far,
    )(*pieces.values())
    return placed[None]


def solution(mesh):
    in_specs = (
        P("rep", None, None),
        P("rep", None, None, None),
        P(None, None, "shard"),
        P("rep", None, None, "shard"),
    )
    out_specs = P(None, None, "shard")
    return jax.shard_map(body, mesh=mesh, in_specs=in_specs, out_specs=out_specs, check_vma=False)
```

```python
import math

import jax
import jax.numpy as jnp
from jax import lax
from jax.experimental import pallas as pl
from jax.experimental.pallas import tpu as pltpu
from jax.sharding import PartitionSpec as P

FF = 512
STEPS = 4
LEARN_RATE = 0.3
MOMENTUM = 0.9
EPSILON = 1e-06
LOADS = 4
VMEM_LIMIT = 48 * 1024 * 1024

F32 = jnp.float32
BF16 = jnp.bfloat16


def reach(steps_between):
    return LEARN_RATE * sum(MOMENTUM**k for k in range(steps_between))


def contract(a, b, dims):
    return lax.dot_general(a, b, (dims, ((), ())), preferred_element_type=F32)


def share_rows(turned_ref, x_ref, distance, out_ref):
    seg = out_ref.shape[1]
    target = lax.axis_index("rep") ^ distance
    held = max(seg, 128)
    at = pl.multiple_of(target * seg // held * held, held)
    moved = jnp.dot(turned_ref[...], x_ref[:, pl.ds(at, held)], preferred_element_type=F32)
    share = moved[:, :seg]
    for place in range(1, held // seg):
        own = target % (held // seg) == place
        share = jnp.where(own, moved[:, place * seg : (place + 1) * seg], share)
    out_ref[...] = share.astype(BF16)


def share_kernel(order, turned_ref, x_ref, *rest):
    for distance, out_ref in zip(order, rest[-len(order) :]):
        share_rows(turned_ref, x_ref, distance, out_ref)


def local_kernel(cut, partner, idx_hbm, pool_hbm, w_hbm, goal_hbm, *rest):
    first_ref, own_ref, turned_ref, x_ref = rest[:4]
    idx_ref, pool_ref, w_ref, goal_ref, sems = rest[4:]
    pool_rows, width = pool_ref.shape
    seg = own_ref.shape[0]
    total_rows = idx_ref.shape[-1]
    batch = total_rows // STEPS
    inv_width = 1.0 / math.sqrt(width)
    inv_batch = 1.0 / math.sqrt(batch)
    share = width // LOADS
    pieces = [pl.ds(n * share, share) for n in range(LOADS)]

    idx_load = pltpu.make_async_copy(
        idx_hbm.at[lax.axis_index("shard") // cut], idx_ref, sems.at[len(pieces) + 2]
    )
    idx_load.start()
    pool_loads = []
    for n in range(LOADS):
        rows = pl.ds(n * (pool_rows // LOADS), pool_rows // LOADS)
        load = pltpu.make_async_copy(pool_hbm.at[rows], pool_ref.at[rows], sems.at[n])
        load.start()
        pool_loads.append(load)
    w_load = pltpu.make_async_copy(w_hbm, w_ref, sems.at[len(pieces)])
    goal_load = pltpu.make_async_copy(goal_hbm, goal_ref, sems.at[len(pieces) + 1])

    idx_load.wait()
    place = lax.broadcasted_iota(jnp.int32, (batch, pool_rows), 1)
    hits = []
    for t in range(STEPS):
        picked = jnp.broadcast_to(idx_ref[:, t * batch : (t + 1) * batch], (8, batch))
        picked = picked.astype(F32).T[:, :1].astype(jnp.int32)
        hits.append(jnp.where(place == picked, 1.0, 0.0).astype(BF16))
    one_hot = jnp.concatenate(hits, axis=0)
    pool_loads[0].wait()
    w_load.start()
    goal_load.start()
    for load in pool_loads[1:]:
        load.wait()
    for piece in pieces:
        x_ref[:, piece] = jnp.dot(
            one_hot, pool_ref[:, piece], preferred_element_type=F32
        ).astype(BF16)
    w_load.wait()
    goal_load.wait()
    base = jnp.dot(x_ref[...], w_ref[...], preferred_element_type=F32) * inv_width

    overlaps = {}
    for s in range(0, STEPS - 1, 2):
        stop = min(s + 2, STEPS - 1)
        overlaps[s] = contract(
            x_ref[(s + 1) * batch :, :], x_ref[s * batch : stop * batch, :], ((1,), (1,))
        )

    spread = []
    for s in range(STEPS - 1):
        first = s // 2 * 2
        halves = []
        for t in range(s + 1, STEPS):
            down, across = (t - first - 1) * batch, (s - first) * batch
            block = overlaps[first][down : down + batch, across : across + batch]
            block = block * (reach(t - s) * inv_batch * inv_width)
            high = block.astype(BF16)
            halves += [high, (block - high.astype(F32)).astype(BF16)]
        spread.append(jnp.concatenate(halves, axis=0))

    hidden = [base[t * batch : (t + 1) * batch] for t in range(STEPS)]
    final = []
    for s in range(STEPS):
        sigma = jax.nn.sigmoid(hidden[s])
        wanted = goal_ref[s * batch : (s + 1) * batch, :].astype(F32)
        grad = (hidden[s] * sigma - wanted) * (sigma * (1.0 + hidden[s] * (1.0 - sigma)))
        if s < STEPS - 1:
            moved = jnp.dot(spread[s], grad.astype(BF16), preferred_element_type=F32)
            for n, t in enumerate(range(s + 1, STEPS)):
                at = 2 * n * batch
                hidden[t] = hidden[t] - (
                    moved[at : at + batch] + moved[at + batch : at + 2 * batch]
                )
        final.append((grad * (-reach(STEPS - s) * inv_batch)).T.astype(BF16))

    turned_ref[...] = jnp.concatenate(final, axis=1)
    share_rows(turned_ref, x_ref, partner, first_ref)
    start = pl.multiple_of(lax.axis_index("rep") * seg, seg)
    own_ref[...] = w_ref[pl.ds(start, seg), :]


def distances(parts):
    def far(distance):
        return (distance == 1, distance & 1, -(distance >> 1).bit_count(), distance)

    return [0, *sorted(range(1, parts), key=far)]


def pair_list(count):
    return [(i, j) for i in range(count) for j in range(i, count)]


def gram_kernel(parts, order, known, *refs):
    count = len(order)
    deltas, before, out_ref = refs[:count], refs[count:-1], refs[-1]
    rows, seg = deltas[0].shape
    lanes = min(128, seg)
    block = min(8, count)
    tall = 16
    me = lax.axis_index("rep")
    down = lax.broadcasted_iota(jnp.int32, out_ref.shape, 0)
    spots = down * 128 + lax.broadcasted_iota(jnp.int32, out_ref.shape, 1)
    table = before[0][...] if before else jnp.zeros(out_ref.shape, F32)
    for first in range(0, count, block):
        for second in range(first, count, block):
            pairs = [
                (i, j)
                for i in range(first, min(first + block, count))
                for j in range(second, min(second + block, count))
                if i <= j and j >= known
            ]
            if not pairs:
                continue
            members = sorted({k for pair in pairs for k in pair})

            def step(at, sums, pairs=pairs, members=members):
                sums = list(sums)
                row = pl.multiple_of(at * tall, tall)
                for lane in range(0, seg, lanes):
                    held = {
                        k: deltas[k][pl.ds(row, tall), lane : lane + lanes].astype(F32)
                        for k in members
                    }
                    for n, (i, j) in enumerate(pairs):
                        product = held[i] * held[j]
                        sums[n] = sums[n] + (product[:8] + product[8:])
                return tuple(sums)

            zeros = tuple(jnp.zeros((8, lanes), F32) for _ in pairs)
            sums = lax.fori_loop(0, rows // tall, step, zeros, unroll=4 if count <= block else 1)
            for n, (i, j) in enumerate(pairs):
                value = jnp.sum(jnp.sum(sums[n], axis=0, keepdims=True), axis=1, keepdims=True)
                mine, other = me ^ order[i], me ^ order[j]
                here = (spots == mine * parts + other) | (spots == other * parts + mine)
                table = jnp.where(here, value, table)
    out_ref[...] = table


def tree_weights(gram, count):
    weights = [None] * count
    current = dict(gram)
    width = 1
    while count > 1:
        left, right = [], []
        for i in range(0, count, 2):
            cross = current[i, i + 1]
            left_square = jnp.maximum(current[i, i], 0.0)
            right_square = jnp.maximum(current[i + 1, i + 1], 0.0)
            left.append(1.0 - cross / (2.0 * (left_square + EPSILON)))
            right.append(1.0 - cross / (2.0 * (right_square + EPSILON)))
        for i in range(count):
            scale = (right if i % 2 else left)[i // 2]
            for k in range(i * width, (i + 1) * width):
                weights[k] = scale if weights[k] is None else weights[k] * scale
        merged = {}
        for i in range(count // 2):
            for j in range(i, count // 2):

                def entry(a, b):
                    return current[min(a, b), max(a, b)]

                merged[i, j] = left[i] * (
                    left[j] * entry(2 * i, 2 * j) + right[j] * entry(2 * i, 2 * j + 1)
                ) + right[i] * (
                    left[j] * entry(2 * i + 1, 2 * j) + right[j] * entry(2 * i + 1, 2 * j + 1)
                )
        current = merged
        count //= 2
        width *= 2
    return weights


def combine_kernel(gram_ref, own_ref, *rest):
    deltas, out_ref = rest[:-1], rest[-1]
    count = len(deltas)
    me = lax.axis_index("rep")
    table = gram_ref[0]
    for member in range(1, gram_ref.shape[0]):
        table = table + gram_ref[member]
    gram = {}
    for i, j in pair_list(count):
        down, across = divmod(i * count + j, 128)
        gram[i, j] = table[down : down + 1, across : across + 1]
    weights = tree_weights(gram, count)
    total = None
    for distance, delta in zip(distances(count), deltas):
        weight = weights[0]
        for k in range(1, count):
            weight = jnp.where((me ^ distance) == k, weights[k], weight)
        term = weight * delta[...].astype(F32)
        total = term if total is None else total + term
    combined = total.T.astype(BF16).astype(F32)
    out_ref[...] = (own_ref[...].astype(F32) + combined).astype(BF16)


def place_kernel(routes, *refs):
    pieces, (out_ref, sems) = refs[:-2], refs[-2:]
    seg = pieces[0].shape[0]
    me = lax.axis_index("rep")
    moves = []
    for n, ((even, odd), piece) in enumerate(zip(routes, pieces)):
        distance = jnp.where(me % 2 == 1, odd, even)
        at = pl.multiple_of((me ^ distance) * seg, seg)
        move = pltpu.make_async_copy(piece, out_ref.at[pl.ds(at, seg)], sems.at[n])
        move.start()
        moves.append(move)
    for move in moves:
        move.wait()


def call(kernel, out_shape, in_specs, scratch=(), out_specs=None):
    extra = {} if out_specs is None else {"out_specs": out_specs}
    return pl.pallas_call(
        kernel,
        out_shape=out_shape,
        in_specs=in_specs,
        scratch_shapes=scratch,
        compiler_params=pltpu.CompilerParams(vmem_limit_bytes=VMEM_LIMIT),
        **extra,
    )


def hold(value):
    return pltpu.with_memory_space_constraint(value, pltpu.HBM)


def flipped(value, replica_bits, shard_bits=0):
    replicas, shards = lax.axis_size("rep"), lax.axis_size("shard")
    bits = replica_bits if isinstance(replica_bits, tuple) else (replica_bits,) * 2
    pairs = [
        (i * shards + j, (i ^ bits[i % 2]) * shards + (j ^ shard_bits))
        for i in range(replicas)
        for j in range(shards)
    ]
    return lax.ppermute(value, ("rep", "shard"), pairs)


def body(token_pool, row_index, weights, targets):
    parts = lax.axis_size("rep")
    width, columns = weights.shape[1:]
    cut = FF // columns
    seg = width // parts
    rows = row_index.shape[-1]
    pool_rows = token_pool.shape[1]
    near = pl.BlockSpec(memory_space=pltpu.VMEM)
    far = pl.BlockSpec(memory_space=pltpu.HBM)
    any_place = pl.BlockSpec(memory_space=pl.ANY)

    order = distances(parts)
    first = order[1]

    def local(*refs):
        local_kernel(cut, first, *refs)

    rows_out = jax.ShapeDtypeStruct((columns, seg), BF16)
    out, own_weights, turned, gathered = call(
        local,
        [
            rows_out,
            jax.ShapeDtypeStruct((seg, columns), BF16),
            jax.ShapeDtypeStruct((columns, rows), BF16),
            jax.ShapeDtypeStruct((rows, width), BF16),
        ],
        [far] * 4,
        [
            pltpu.VMEM((1, rows), jnp.int32),
            pltpu.VMEM((pool_rows, width), BF16),
            pltpu.VMEM((width, columns), BF16),
            pltpu.VMEM((rows, columns), BF16),
            pltpu.SemaphoreType.DMA((LOADS + 3,)),
        ],
    )(hold(row_index[0]), hold(token_pool[0]), hold(weights[0]), hold(targets[0, 0]))
    leaves = {first: flipped(out, first)}
    middle = max(2, parts - 2)
    for group, after in (
        ([0, *order[2:middle]], []),
        (order[middle:], [leaves[first]]),
    ):
        if not group:
            continue

        def shares(*refs, group=group):
            share_kernel(group, *refs)

        made = call(shares, [rows_out] * len(group), [near] * (2 + len(after)))(
            turned, gathered, *after
        )
        for d, out in zip(group, made):
            leaves[d] = flipped(out, d) if d else out

    table = jax.ShapeDtypeStruct((-(-parts * parts // 128), 128), F32)
    gram, known = [], 0
    for reached in (parts - 3, parts - 2, parts):
        if reached <= known:
            continue
        taken = order[:reached]

        def products(*refs, taken=taken, known=known):
            gram_kernel(parts, taken, known, *refs)

        inputs = [leaves[d] for d in taken] + gram
        gram, known = [call(products, table, [near] * len(inputs))(*inputs)], reached
    gram = gram[0]
    shards = lax.axis_size("shard")
    groups = [
        [i * shards + j for i in range(parts) for j in range(first, first + cut)]
        for first in range(0, shards, cut)
    ]
    groups = [group[::-1] for group in groups]
    gram = jnp.broadcast_to(gram, (parts * cut, *gram.shape))
    gram = lax.all_to_all(gram, ("rep", "shard"), 0, 0, axis_index_groups=groups)

    own = call(
        combine_kernel,
        jax.ShapeDtypeStruct((seg, columns), BF16),
        [near] * (parts + 2),
    )(gram, own_weights, *(leaves[d] for d in order))
    pieces = {(0, 0): own, (1, 1): flipped(own, 1)}
    bits = parts.bit_length() - 2
    for chip in range(parts // 2 - 1, 0, -1):
        mirror = sum((chip >> k & 1) << (bits - 1 - k) for k in range(bits))
        if mirror == chip:
            came, passed = (2 * chip, 2 * chip), (2 * chip + 1, 2 * chip + 1)
        else:
            came, passed = (2 * chip, 2 * mirror), (2 * mirror + 1, 2 * chip + 1)
        pieces[came] = flipped(own, came)
        pieces[passed] = flipped(pieces[came], 1)

    def place(*refs):
        place_kernel(list(pieces), *refs)

    placed = call(
        place,
        jax.ShapeDtypeStruct((width, columns), BF16),
        [any_place] * parts,
        [pltpu.SemaphoreType.DMA((parts,))],
        far,
    )(*pieces.values())
    return placed[None]


def solution(mesh):
    in_specs = (
        P("rep", None, None),
        P("rep", None, None, None),
        P(None, None, "shard"),
        P("rep", None, None, "shard"),
    )
    out_specs = P(None, None, "shard")
    return jax.shard_map(body, mesh=mesh, in_specs=in_specs, out_specs=out_specs, check_vma=False)
```

```python
import math

import jax
import jax.numpy as jnp
from jax import lax
from jax.experimental import pallas as pl
from jax.experimental.pallas import tpu as pltpu
from jax.sharding import PartitionSpec as P

FF = 512
STEPS = 4
LEARN_RATE = 0.3
MOMENTUM = 0.9
EPSILON = 1e-06
LOADS = 4
VMEM_LIMIT = 48 * 1024 * 1024

F32 = jnp.float32
BF16 = jnp.bfloat16


def reach(steps_between):
    return LEARN_RATE * sum(MOMENTUM**k for k in range(steps_between))


def contract(a, b, dims):
    return lax.dot_general(a, b, (dims, ((), ())), preferred_element_type=F32)


def share_rows(turned_ref, x_ref, distance, out_ref):
    seg = out_ref.shape[1]
    target = lax.axis_index("rep") ^ distance
    held = max(seg, 128)
    at = pl.multiple_of(target * seg // held * held, held)
    moved = jnp.dot(turned_ref[...], x_ref[:, pl.ds(at, held)], preferred_element_type=F32)
    share = moved[:, :seg]
    for place in range(1, held // seg):
        own = target % (held // seg) == place
        share = jnp.where(own, moved[:, place * seg : (place + 1) * seg], share)
    out_ref[...] = share.astype(BF16)


def share_kernel(order, turned_ref, x_ref, *rest):
    for distance, out_ref in zip(order, rest[-len(order) :]):
        share_rows(turned_ref, x_ref, distance, out_ref)


def local_kernel(cut, partner, idx_hbm, pool_hbm, w_hbm, goal_hbm, *rest):
    first_ref, own_ref, turned_ref, x_ref = rest[:4]
    idx_ref, pool_ref, w_ref, goal_ref, sems = rest[4:]
    pool_rows, width = pool_ref.shape
    seg = own_ref.shape[0]
    total_rows = idx_ref.shape[-1]
    batch = total_rows // STEPS
    inv_width = 1.0 / math.sqrt(width)
    inv_batch = 1.0 / math.sqrt(batch)
    share = width // LOADS
    pieces = [pl.ds(n * share, share) for n in range(LOADS)]

    idx_load = pltpu.make_async_copy(
        idx_hbm.at[lax.axis_index("shard") // cut], idx_ref, sems.at[len(pieces) + 2]
    )
    idx_load.start()
    pool_loads = []
    for n in range(LOADS):
        rows = pl.ds(n * (pool_rows // LOADS), pool_rows // LOADS)
        load = pltpu.make_async_copy(pool_hbm.at[rows], pool_ref.at[rows], sems.at[n])
        load.start()
        pool_loads.append(load)
    w_load = pltpu.make_async_copy(w_hbm, w_ref, sems.at[len(pieces)])
    goal_load = pltpu.make_async_copy(goal_hbm, goal_ref, sems.at[len(pieces) + 1])

    idx_load.wait()
    place = lax.broadcasted_iota(jnp.int32, (batch, pool_rows), 1)
    hits = []
    for t in range(STEPS):
        picked = jnp.broadcast_to(idx_ref[:, t * batch : (t + 1) * batch], (8, batch))
        picked = picked.astype(F32).T[:, :1].astype(jnp.int32)
        hits.append(jnp.where(place == picked, 1.0, 0.0).astype(BF16))
    one_hot = jnp.concatenate(hits, axis=0)
    pool_loads[0].wait()
    w_load.start()
    goal_load.start()
    for load in pool_loads[1:]:
        load.wait()
    for piece in pieces:
        x_ref[:, piece] = jnp.dot(
            one_hot, pool_ref[:, piece], preferred_element_type=F32
        ).astype(BF16)
    w_load.wait()
    goal_load.wait()
    base = jnp.dot(x_ref[...], w_ref[...], preferred_element_type=F32) * inv_width

    overlaps = {}
    for s in range(0, STEPS - 1, 2):
        stop = min(s + 2, STEPS - 1)
        overlaps[s] = contract(
            x_ref[(s + 1) * batch :, :], x_ref[s * batch : stop * batch, :], ((1,), (1,))
        )

    spread = []
    for s in range(STEPS - 1):
        first = s // 2 * 2
        halves = []
        for t in range(s + 1, STEPS):
            down, across = (t - first - 1) * batch, (s - first) * batch
            block = overlaps[first][down : down + batch, across : across + batch]
            block = block * (reach(t - s) * inv_batch * inv_width)
            high = block.astype(BF16)
            halves += [high, (block - high.astype(F32)).astype(BF16)]
        spread.append(jnp.concatenate(halves, axis=0))

    hidden = [base[t * batch : (t + 1) * batch] for t in range(STEPS)]
    final = []
    for s in range(STEPS):
        sigma = jax.nn.sigmoid(hidden[s])
        wanted = goal_ref[s * batch : (s + 1) * batch, :].astype(F32)
        grad = (hidden[s] * sigma - wanted) * (sigma * (1.0 + hidden[s] * (1.0 - sigma)))
        if s < STEPS - 1:
            moved = jnp.dot(spread[s], grad.astype(BF16), preferred_element_type=F32)
            for n, t in enumerate(range(s + 1, STEPS)):
                at = 2 * n * batch
                hidden[t] = hidden[t] - (
                    moved[at : at + batch] + moved[at + batch : at + 2 * batch]
                )
        final.append((grad * (-reach(STEPS - s) * inv_batch)).T.astype(BF16))

    turned_ref[...] = jnp.concatenate(final, axis=1)
    share_rows(turned_ref, x_ref, partner, first_ref)
    start = pl.multiple_of(lax.axis_index("rep") * seg, seg)
    own_ref[...] = w_ref[pl.ds(start, seg), :]


def distances(parts):
    def far(distance):
        return (distance == 1, -(distance >> 1).bit_count(), distance & 1, distance)

    return [0, *sorted(range(1, parts), key=far)]


def pair_list(count):
    return [(i, j) for i in range(count) for j in range(i, count)]


def gram_kernel(parts, order, known, *refs):
    count = len(order)
    deltas, before, out_ref = refs[:count], refs[count:-1], refs[-1]
    rows, seg = deltas[0].shape
    lanes = min(128, seg)
    block = min(8, count)
    tall = 16
    me = lax.axis_index("rep")
    down = lax.broadcasted_iota(jnp.int32, out_ref.shape, 0)
    spots = down * 128 + lax.broadcasted_iota(jnp.int32, out_ref.shape, 1)
    table = before[0][...] if before else jnp.zeros(out_ref.shape, F32)
    for first in range(0, count, block):
        for second in range(first, count, block):
            pairs = [
                (i, j)
                for i in range(first, min(first + block, count))
                for j in range(second, min(second + block, count))
                if i <= j and j >= known
            ]
            if not pairs:
                continue
            members = sorted({k for pair in pairs for k in pair})

            def step(at, sums, pairs=pairs, members=members):
                sums = list(sums)
                row = pl.multiple_of(at * tall, tall)
                for lane in range(0, seg, lanes):
                    held = {
                        k: deltas[k][pl.ds(row, tall), lane : lane + lanes].astype(F32)
                        for k in members
                    }
                    for n, (i, j) in enumerate(pairs):
                        product = held[i] * held[j]
                        sums[n] = sums[n] + (product[:8] + product[8:])
                return tuple(sums)

            zeros = tuple(jnp.zeros((8, lanes), F32) for _ in pairs)
            sums = lax.fori_loop(0, rows // tall, step, zeros, unroll=4 if count <= block else 1)
            for n, (i, j) in enumerate(pairs):
                value = jnp.sum(jnp.sum(sums[n], axis=0, keepdims=True), axis=1, keepdims=True)
                mine, other = me ^ order[i], me ^ order[j]
                here = (spots == mine * parts + other) | (spots == other * parts + mine)
                table = jnp.where(here, value, table)
    out_ref[...] = table


def tree_weights(gram, count):
    weights = [None] * count
    current = dict(gram)
    width = 1
    while count > 1:
        left, right = [], []
        for i in range(0, count, 2):
            cross = current[i, i + 1]
            left_square = jnp.maximum(current[i, i], 0.0)
            right_square = jnp.maximum(current[i + 1, i + 1], 0.0)
            left.append(1.0 - cross / (2.0 * (left_square + EPSILON)))
            right.append(1.0 - cross / (2.0 * (right_square + EPSILON)))
        for i in range(count):
            scale = (right if i % 2 else left)[i // 2]
            for k in range(i * width, (i + 1) * width):
                weights[k] = scale if weights[k] is None else weights[k] * scale
        merged = {}
        for i in range(count // 2):
            for j in range(i, count // 2):

                def entry(a, b):
                    return current[min(a, b), max(a, b)]

                merged[i, j] = left[i] * (
                    left[j] * entry(2 * i, 2 * j) + right[j] * entry(2 * i, 2 * j + 1)
                ) + right[i] * (
                    left[j] * entry(2 * i + 1, 2 * j) + right[j] * entry(2 * i + 1, 2 * j + 1)
                )
        current = merged
        count //= 2
        width *= 2
    return weights


def combine_kernel(gram_ref, own_ref, *rest):
    deltas, out_ref = rest[:-1], rest[-1]
    count = len(deltas)
    me = lax.axis_index("rep")
    table = gram_ref[0]
    for member in range(1, gram_ref.shape[0]):
        table = table + gram_ref[member]
    gram = {}
    for i, j in pair_list(count):
        down, across = divmod(i * count + j, 128)
        gram[i, j] = table[down : down + 1, across : across + 1]
    weights = tree_weights(gram, count)
    total = None
    for distance, delta in zip(distances(count), deltas):
        weight = weights[0]
        for k in range(1, count):
            weight = jnp.where((me ^ distance) == k, weights[k], weight)
        term = weight * delta[...].astype(F32)
        total = term if total is None else total + term
    combined = total.T.astype(BF16).astype(F32)
    out_ref[...] = (own_ref[...].astype(F32) + combined).astype(BF16)


def place_kernel(routes, *refs):
    pieces, (out_ref, sems) = refs[:-2], refs[-2:]
    seg = pieces[0].shape[0]
    me = lax.axis_index("rep")
    moves = []
    for n, ((even, odd), piece) in enumerate(zip(routes, pieces)):
        distance = jnp.where(me % 2 == 1, odd, even)
        at = pl.multiple_of((me ^ distance) * seg, seg)
        move = pltpu.make_async_copy(piece, out_ref.at[pl.ds(at, seg)], sems.at[n])
        move.start()
        moves.append(move)
    for move in moves:
        move.wait()


def call(kernel, out_shape, in_specs, scratch=(), out_specs=None):
    extra = {} if out_specs is None else {"out_specs": out_specs}
    return pl.pallas_call(
        kernel,
        out_shape=out_shape,
        in_specs=in_specs,
        scratch_shapes=scratch,
        compiler_params=pltpu.CompilerParams(vmem_limit_bytes=VMEM_LIMIT),
        **extra,
    )


def hold(value):
    return pltpu.with_memory_space_constraint(value, pltpu.HBM)


def flipped(value, replica_bits, shard_bits=0):
    replicas, shards = lax.axis_size("rep"), lax.axis_size("shard")
    bits = replica_bits if isinstance(replica_bits, tuple) else (replica_bits,) * 2
    pairs = [
        (i * shards + j, (i ^ bits[i % 2]) * shards + (j ^ shard_bits))
        for i in range(replicas)
        for j in range(shards)
    ]
    return lax.ppermute(value, ("rep", "shard"), pairs)


def body(token_pool, row_index, weights, targets):
    parts = lax.axis_size("rep")
    width, columns = weights.shape[1:]
    cut = FF // columns
    seg = width // parts
    rows = row_index.shape[-1]
    pool_rows = token_pool.shape[1]
    near = pl.BlockSpec(memory_space=pltpu.VMEM)
    far = pl.BlockSpec(memory_space=pltpu.HBM)
    any_place = pl.BlockSpec(memory_space=pl.ANY)

    order = distances(parts)
    first = order[1]

    def local(*refs):
        local_kernel(cut, first, *refs)

    rows_out = jax.ShapeDtypeStruct((columns, seg), BF16)
    out, own_weights, turned, gathered = call(
        local,
        [
            rows_out,
            jax.ShapeDtypeStruct((seg, columns), BF16),
            jax.ShapeDtypeStruct((columns, rows), BF16),
            jax.ShapeDtypeStruct((rows, width), BF16),
        ],
        [far] * 4,
        [
            pltpu.VMEM((1, rows), jnp.int32),
            pltpu.VMEM((pool_rows, width), BF16),
            pltpu.VMEM((width, columns), BF16),
            pltpu.VMEM((rows, columns), BF16),
            pltpu.SemaphoreType.DMA((LOADS + 3,)),
        ],
    )(hold(row_index[0]), hold(token_pool[0]), hold(weights[0]), hold(targets[0, 0]))
    leaves = {first: flipped(out, first)}
    middle = max(2, parts - 2)
    for group, after in (
        ([0, *order[2:middle]], []),
        (order[middle:], [leaves[first]]),
    ):
        if not group:
            continue

        def shares(*refs, group=group):
            share_kernel(group, *refs)

        made = call(shares, [rows_out] * len(group), [near] * (2 + len(after)))(
            turned, gathered, *after
        )
        for d, out in zip(group, made):
            leaves[d] = flipped(out, d) if d else out

    table = jax.ShapeDtypeStruct((-(-parts * parts // 128), 128), F32)
    gram, known = [], 0
    for reached in (parts - 3, parts - 2, parts):
        if reached <= known:
            continue
        taken = order[:reached]

        def products(*refs, taken=taken, known=known):
            gram_kernel(parts, taken, known, *refs)

        inputs = [leaves[d] for d in taken] + gram
        gram, known = [call(products, table, [near] * len(inputs))(*inputs)], reached
    gram = gram[0]
    shards = lax.axis_size("shard")
    groups = [
        [i * shards + j for i in range(parts) for j in range(first, first + cut)]
        for first in range(0, shards, cut)
    ]
    groups = [group[::-1] for group in groups]
    gram = jnp.broadcast_to(gram, (parts * cut, *gram.shape))
    gram = lax.all_to_all(gram, ("rep", "shard"), 0, 0, axis_index_groups=groups)

    own = call(
        combine_kernel,
        jax.ShapeDtypeStruct((seg, columns), BF16),
        [near] * (parts + 2),
    )(gram, own_weights, *(leaves[d] for d in order))
    pieces = {(0, 0): own, (1, 1): flipped(own, 1)}
    bits = parts.bit_length() - 2
    for chip in range(parts // 2 - 1, 0, -1):
        mirror = sum((chip >> k & 1) << (bits - 1 - k) for k in range(bits))
        if mirror == chip:
            came, passed = (2 * chip + 1, 2 * chip + 1), (2 * chip, 2 * chip)
        else:
            came, passed = (2 * chip, 2 * mirror), (2 * mirror + 1, 2 * chip + 1)
        pieces[came] = flipped(own, came)
        pieces[passed] = flipped(pieces[came], 1)

    def place(*refs):
        place_kernel(list(pieces), *refs)

    placed = call(
        place,
        jax.ShapeDtypeStruct((width, columns), BF16),
        [any_place] * parts,
        [pltpu.SemaphoreType.DMA((parts,))],
        far,
    )(*pieces.values())
    return placed[None]


def solution(mesh):
    in_specs = (
        P("rep", None, None),
        P("rep", None, None, None),
        P(None, None, "shard"),
        P("rep", None, None, "shard"),
    )
    out_specs = P(None, None, "shard")
    return jax.shard_map(body, mesh=mesh, in_specs=in_specs, out_specs=out_specs, check_vma=False)
```

```python
import math

import jax
import jax.numpy as jnp
from jax import lax
from jax.experimental import pallas as pl
from jax.experimental.pallas import tpu as pltpu
from jax.sharding import PartitionSpec as P

FF = 512
STEPS = 4
LEARN_RATE = 0.3
MOMENTUM = 0.9
EPSILON = 1e-06
LOADS = 4
VMEM_LIMIT = 48 * 1024 * 1024

F32 = jnp.float32
BF16 = jnp.bfloat16


def reach(steps_between):
    return LEARN_RATE * sum(MOMENTUM**k for k in range(steps_between))


def contract(a, b, dims):
    return lax.dot_general(a, b, (dims, ((), ())), preferred_element_type=F32)


def share_rows(turned_ref, x_ref, distance, out_ref):
    seg = out_ref.shape[1]
    target = lax.axis_index("rep") ^ distance
    held = max(seg, 128)
    at = pl.multiple_of(target * seg // held * held, held)
    moved = jnp.dot(turned_ref[...], x_ref[:, pl.ds(at, held)], preferred_element_type=F32)
    share = moved[:, :seg]
    for place in range(1, held // seg):
        own = target % (held // seg) == place
        share = jnp.where(own, moved[:, place * seg : (place + 1) * seg], share)
    out_ref[...] = share.astype(BF16)


def share_kernel(order, turned_ref, x_ref, *rest):
    for distance, out_ref in zip(order, rest[-len(order) :]):
        share_rows(turned_ref, x_ref, distance, out_ref)


def local_kernel(cut, partner, idx_hbm, pool_hbm, w_hbm, goal_hbm, *rest):
    first_ref, own_ref, turned_ref, x_ref = rest[:4]
    idx_ref, pool_ref, w_ref, goal_ref, sems = rest[4:]
    pool_rows, width = pool_ref.shape
    seg = own_ref.shape[0]
    total_rows = idx_ref.shape[-1]
    batch = total_rows // STEPS
    inv_width = 1.0 / math.sqrt(width)
    inv_batch = 1.0 / math.sqrt(batch)
    share = width // LOADS
    pieces = [pl.ds(n * share, share) for n in range(LOADS)]

    idx_load = pltpu.make_async_copy(
        idx_hbm.at[lax.axis_index("shard") // cut], idx_ref, sems.at[len(pieces) + 2]
    )
    idx_load.start()
    pool_loads = []
    for n in range(LOADS):
        rows = pl.ds(n * (pool_rows // LOADS), pool_rows // LOADS)
        load = pltpu.make_async_copy(pool_hbm.at[rows], pool_ref.at[rows], sems.at[n])
        load.start()
        pool_loads.append(load)
    w_load = pltpu.make_async_copy(w_hbm, w_ref, sems.at[len(pieces)])
    goal_load = pltpu.make_async_copy(goal_hbm, goal_ref, sems.at[len(pieces) + 1])

    idx_load.wait()
    place = lax.broadcasted_iota(jnp.int32, (batch, pool_rows), 1)
    hits = []
    for t in range(STEPS):
        picked = jnp.broadcast_to(idx_ref[:, t * batch : (t + 1) * batch], (8, batch))
        picked = picked.astype(F32).T[:, :1].astype(jnp.int32)
        hits.append(jnp.where(place == picked, 1.0, 0.0).astype(BF16))
    one_hot = jnp.concatenate(hits, axis=0)
    pool_loads[0].wait()
    w_load.start()
    goal_load.start()
    for load in pool_loads[1:]:
        load.wait()
    for piece in pieces:
        x_ref[:, piece] = jnp.dot(
            one_hot, pool_ref[:, piece], preferred_element_type=F32
        ).astype(BF16)
    w_load.wait()
    goal_load.wait()
    base = jnp.dot(x_ref[...], w_ref[...], preferred_element_type=F32) * inv_width

    overlaps = {}
    for s in range(0, STEPS - 1, 2):
        stop = min(s + 2, STEPS - 1)
        overlaps[s] = contract(
            x_ref[(s + 1) * batch :, :], x_ref[s * batch : stop * batch, :], ((1,), (1,))
        )

    spread = []
    for s in range(STEPS - 1):
        first = s // 2 * 2
        halves = []
        for t in range(s + 1, STEPS):
            down, across = (t - first - 1) * batch, (s - first) * batch
            block = overlaps[first][down : down + batch, across : across + batch]
            block = block * (reach(t - s) * inv_batch * inv_width)
            high = block.astype(BF16)
            halves += [high, (block - high.astype(F32)).astype(BF16)]
        spread.append(jnp.concatenate(halves, axis=0))

    hidden = [base[t * batch : (t + 1) * batch] for t in range(STEPS)]
    final = []
    for s in range(STEPS):
        sigma = jax.nn.sigmoid(hidden[s])
        wanted = goal_ref[s * batch : (s + 1) * batch, :].astype(F32)
        grad = (hidden[s] * sigma - wanted) * (sigma * (1.0 + hidden[s] * (1.0 - sigma)))
        if s < STEPS - 1:
            moved = jnp.dot(spread[s], grad.astype(BF16), preferred_element_type=F32)
            for n, t in enumerate(range(s + 1, STEPS)):
                at = 2 * n * batch
                hidden[t] = hidden[t] - (
                    moved[at : at + batch] + moved[at + batch : at + 2 * batch]
                )
        final.append((grad * (-reach(STEPS - s) * inv_batch)).T.astype(BF16))

    turned_ref[...] = jnp.concatenate(final, axis=1)
    share_rows(turned_ref, x_ref, partner, first_ref)
    start = pl.multiple_of(lax.axis_index("rep") * seg, seg)
    own_ref[...] = w_ref[pl.ds(start, seg), :]


def distances(parts):
    def far(distance):
        return (distance == 1, distance & 1, -(distance >> 1).bit_count(), distance)

    return [0, *sorted(range(1, parts), key=far)]


def pair_list(count):
    return [(i, j) for i in range(count) for j in range(i, count)]


def gram_kernel(parts, order, known, *refs):
    count = len(order)
    deltas, before, out_ref = refs[:count], refs[count:-1], refs[-1]
    rows, seg = deltas[0].shape
    lanes = min(128, seg)
    block = min(8, count)
    tall = 16
    me = lax.axis_index("rep")
    down = lax.broadcasted_iota(jnp.int32, out_ref.shape, 0)
    spots = down * 128 + lax.broadcasted_iota(jnp.int32, out_ref.shape, 1)
    table = before[0][...] if before else jnp.zeros(out_ref.shape, F32)
    for first in range(0, count, block):
        for second in range(first, count, block):
            pairs = [
                (i, j)
                for i in range(first, min(first + block, count))
                for j in range(second, min(second + block, count))
                if i <= j and j >= known
            ]
            if not pairs:
                continue
            members = sorted({k for pair in pairs for k in pair})

            def step(at, sums, pairs=pairs, members=members):
                sums = list(sums)
                row = pl.multiple_of(at * tall, tall)
                for lane in range(0, seg, lanes):
                    held = {
                        k: deltas[k][pl.ds(row, tall), lane : lane + lanes].astype(F32)
                        for k in members
                    }
                    for n, (i, j) in enumerate(pairs):
                        product = held[i] * held[j]
                        sums[n] = sums[n] + (product[:8] + product[8:])
                return tuple(sums)

            zeros = tuple(jnp.zeros((8, lanes), F32) for _ in pairs)
            sums = lax.fori_loop(0, rows // tall, step, zeros, unroll=4 if count <= block else 1)
            for n, (i, j) in enumerate(pairs):
                value = jnp.sum(jnp.sum(sums[n], axis=0, keepdims=True), axis=1, keepdims=True)
                mine, other = me ^ order[i], me ^ order[j]
                here = (spots == mine * parts + other) | (spots == other * parts + mine)
                table = jnp.where(here, value, table)
    out_ref[...] = table


def tree_weights(gram, count):
    weights = [None] * count
    current = dict(gram)
    width = 1
    while count > 1:
        left, right = [], []
        for i in range(0, count, 2):
            cross = current[i, i + 1]
            left_square = jnp.maximum(current[i, i], 0.0)
            right_square = jnp.maximum(current[i + 1, i + 1], 0.0)
            left.append(1.0 - cross / (2.0 * (left_square + EPSILON)))
            right.append(1.0 - cross / (2.0 * (right_square + EPSILON)))
        for i in range(count):
            scale = (right if i % 2 else left)[i // 2]
            for k in range(i * width, (i + 1) * width):
                weights[k] = scale if weights[k] is None else weights[k] * scale
        merged = {}
        for i in range(count // 2):
            for j in range(i, count // 2):

                def entry(a, b):
                    return current[min(a, b), max(a, b)]

                merged[i, j] = left[i] * (
                    left[j] * entry(2 * i, 2 * j) + right[j] * entry(2 * i, 2 * j + 1)
                ) + right[i] * (
                    left[j] * entry(2 * i + 1, 2 * j) + right[j] * entry(2 * i + 1, 2 * j + 1)
                )
        current = merged
        count //= 2
        width *= 2
    return weights


def combine_kernel(gram_ref, own_ref, *rest):
    deltas, out_ref = rest[:-1], rest[-1]
    count = len(deltas)
    me = lax.axis_index("rep")
    table = gram_ref[0]
    for member in range(1, gram_ref.shape[0]):
        table = table + gram_ref[member]
    gram = {}
    for i, j in pair_list(count):
        down, across = divmod(i * count + j, 128)
        gram[i, j] = table[down : down + 1, across : across + 1]
    weights = tree_weights(gram, count)
    total = None
    for distance, delta in zip(distances(count), deltas):
        weight = weights[0]
        for k in range(1, count):
            weight = jnp.where((me ^ distance) == k, weights[k], weight)
        term = weight * delta[...].astype(F32)
        total = term if total is None else total + term
    combined = total.T.astype(BF16).astype(F32)
    out_ref[...] = (own_ref[...].astype(F32) + combined).astype(BF16)


def place_kernel(routes, *refs):
    pieces, (out_ref, sems) = refs[:-2], refs[-2:]
    seg = pieces[0].shape[0]
    me = lax.axis_index("rep")
    moves = []
    for n, ((even, odd), piece) in enumerate(zip(routes, pieces)):
        distance = jnp.where(me % 2 == 1, odd, even)
        at = pl.multiple_of((me ^ distance) * seg, seg)
        move = pltpu.make_async_copy(piece, out_ref.at[pl.ds(at, seg)], sems.at[n])
        move.start()
        moves.append(move)
    for move in moves:
        move.wait()


def call(kernel, out_shape, in_specs, scratch=(), out_specs=None):
    extra = {} if out_specs is None else {"out_specs": out_specs}
    return pl.pallas_call(
        kernel,
        out_shape=out_shape,
        in_specs=in_specs,
        scratch_shapes=scratch,
        compiler_params=pltpu.CompilerParams(vmem_limit_bytes=VMEM_LIMIT),
        **extra,
    )


def hold(value):
    return pltpu.with_memory_space_constraint(value, pltpu.HBM)


def flipped(value, replica_bits, shard_bits=0):
    replicas, shards = lax.axis_size("rep"), lax.axis_size("shard")
    bits = replica_bits if isinstance(replica_bits, tuple) else (replica_bits,) * 2
    pairs = [
        (i * shards + j, (i ^ bits[i % 2]) * shards + (j ^ shard_bits))
        for i in range(replicas)
        for j in range(shards)
    ]
    return lax.ppermute(value, ("rep", "shard"), pairs)


def body(token_pool, row_index, weights, targets):
    parts = lax.axis_size("rep")
    width, columns = weights.shape[1:]
    cut = FF // columns
    seg = width // parts
    rows = row_index.shape[-1]
    pool_rows = token_pool.shape[1]
    near = pl.BlockSpec(memory_space=pltpu.VMEM)
    far = pl.BlockSpec(memory_space=pltpu.HBM)
    any_place = pl.BlockSpec(memory_space=pl.ANY)

    order = distances(parts)
    first = order[1]

    def local(*refs):
        local_kernel(cut, first, *refs)

    rows_out = jax.ShapeDtypeStruct((columns, seg), BF16)
    out, own_weights, turned, gathered = call(
        local,
        [
            rows_out,
            jax.ShapeDtypeStruct((seg, columns), BF16),
            jax.ShapeDtypeStruct((columns, rows), BF16),
            jax.ShapeDtypeStruct((rows, width), BF16),
        ],
        [far] * 4,
        [
            pltpu.VMEM((1, rows), jnp.int32),
            pltpu.VMEM((pool_rows, width), BF16),
            pltpu.VMEM((width, columns), BF16),
            pltpu.VMEM((rows, columns), BF16),
            pltpu.SemaphoreType.DMA((LOADS + 3,)),
        ],
    )(hold(row_index[0]), hold(token_pool[0]), hold(weights[0]), hold(targets[0, 0]))
    leaves = {first: flipped(out, first)}
    middle = max(2, parts - 2)
    for group, after in (
        ([0, *order[2:middle]], []),
        (order[middle:], [leaves[first]]),
    ):
        if not group:
            continue

        def shares(*refs, group=group):
            share_kernel(group, *refs)

        made = call(shares, [rows_out] * len(group), [near] * (2 + len(after)))(
            turned, gathered, *after
        )
        for d, out in zip(group, made):
            leaves[d] = flipped(out, d) if d else out

    table = jax.ShapeDtypeStruct((-(-parts * parts // 128), 128), F32)
    gram, known = [], 0
    for reached in (parts - 3, parts - 2, parts):
        if reached <= known:
            continue
        taken = order[:reached]

        def products(*refs, taken=taken, known=known):
            gram_kernel(parts, taken, known, *refs)

        inputs = [leaves[d] for d in taken] + gram
        gram, known = [call(products, table, [near] * len(inputs))(*inputs)], reached
    gram = gram[0]
    shards = lax.axis_size("shard")
    groups = [
        [i * shards + j for j in range(first, first + cut) for i in range(parts)]
        for first in range(0, shards, cut)
    ]
    groups = [group[::-1] for group in groups]
    gram = jnp.broadcast_to(gram, (parts * cut, *gram.shape))
    gram = lax.all_to_all(gram, ("rep", "shard"), 0, 0, axis_index_groups=groups)

    own = call(
        combine_kernel,
        jax.ShapeDtypeStruct((seg, columns), BF16),
        [near] * (parts + 2),
    )(gram, own_weights, *(leaves[d] for d in order))
    pieces = {(0, 0): own, (1, 1): flipped(own, 1)}
    bits = parts.bit_length() - 2
    for chip in range(parts // 2 - 1, 0, -1):
        mirror = sum((chip >> k & 1) << (bits - 1 - k) for k in range(bits))
        if mirror == chip:
            came, passed = (2 * chip + 1, 2 * chip + 1), (2 * chip, 2 * chip)
        else:
            came, passed = (2 * chip, 2 * mirror), (2 * mirror + 1, 2 * chip + 1)
        pieces[came] = flipped(own, came)
        pieces[passed] = flipped(pieces[came], 1)

    def place(*refs):
        place_kernel(list(pieces), *refs)

    placed = call(
        place,
        jax.ShapeDtypeStruct((width, columns), BF16),
        [any_place] * parts,
        [pltpu.SemaphoreType.DMA((parts,))],
        far,
    )(*pieces.values())
    return placed[None]


def solution(mesh):
    in_specs = (
        P("rep", None, None),
        P("rep", None, None, None),
        P(None, None, "shard"),
        P("rep", None, None, "shard"),
    )
    out_specs = P(None, None, "shard")
    return jax.shard_map(body, mesh=mesh, in_specs=in_specs, out_specs=out_specs, check_vma=False)
```

```python
import math

import jax
import jax.numpy as jnp
from jax import lax
from jax.experimental import pallas as pl
from jax.experimental.pallas import tpu as pltpu
from jax.sharding import PartitionSpec as P

FF = 512
STEPS = 4
LEARN_RATE = 0.3
MOMENTUM = 0.9
EPSILON = 1e-06
LOADS = 4
VMEM_LIMIT = 48 * 1024 * 1024

F32 = jnp.float32
BF16 = jnp.bfloat16


def reach(steps_between):
    return LEARN_RATE * sum(MOMENTUM**k for k in range(steps_between))


def contract(a, b, dims):
    return lax.dot_general(a, b, (dims, ((), ())), preferred_element_type=F32)


def share_rows(turned_ref, x_ref, distance, out_ref):
    seg = out_ref.shape[1]
    target = lax.axis_index("rep") ^ distance
    held = max(seg, 128)
    at = pl.multiple_of(target * seg // held * held, held)
    moved = jnp.dot(turned_ref[...], x_ref[:, pl.ds(at, held)], preferred_element_type=F32)
    share = moved[:, :seg]
    for place in range(1, held // seg):
        own = target % (held // seg) == place
        share = jnp.where(own, moved[:, place * seg : (place + 1) * seg], share)
    out_ref[...] = share.astype(BF16)


def share_kernel(order, turned_ref, x_ref, *rest):
    for distance, out_ref in zip(order, rest[-len(order) :]):
        share_rows(turned_ref, x_ref, distance, out_ref)


def local_kernel(cut, partner, idx_hbm, pool_hbm, w_hbm, goal_hbm, *rest):
    first_ref, own_ref, turned_ref, x_ref = rest[:4]
    idx_ref, pool_ref, w_ref, goal_ref, sems = rest[4:]
    pool_rows, width = pool_ref.shape
    seg = own_ref.shape[0]
    total_rows = idx_ref.shape[-1]
    batch = total_rows // STEPS
    inv_width = 1.0 / math.sqrt(width)
    inv_batch = 1.0 / math.sqrt(batch)
    share = width // LOADS
    pieces = [pl.ds(n * share, share) for n in range(LOADS)]

    idx_load = pltpu.make_async_copy(
        idx_hbm.at[lax.axis_index("shard") // cut], idx_ref, sems.at[len(pieces) + 2]
    )
    idx_load.start()
    pool_loads = []
    for n in range(LOADS):
        rows = pl.ds(n * (pool_rows // LOADS), pool_rows // LOADS)
        load = pltpu.make_async_copy(pool_hbm.at[rows], pool_ref.at[rows], sems.at[n])
        load.start()
        pool_loads.append(load)
    w_load = pltpu.make_async_copy(w_hbm, w_ref, sems.at[len(pieces)])
    goal_load = pltpu.make_async_copy(goal_hbm, goal_ref, sems.at[len(pieces) + 1])

    idx_load.wait()
    place = lax.broadcasted_iota(jnp.int32, (batch, pool_rows), 1)
    hits = []
    for t in range(STEPS):
        picked = jnp.broadcast_to(idx_ref[:, t * batch : (t + 1) * batch], (8, batch))
        picked = picked.astype(F32).T[:, :1].astype(jnp.int32)
        hits.append(jnp.where(place == picked, 1.0, 0.0).astype(BF16))
    one_hot = jnp.concatenate(hits, axis=0)
    pool_loads[0].wait()
    w_load.start()
    goal_load.start()
    for load in pool_loads[1:]:
        load.wait()
    for piece in pieces:
        x_ref[:, piece] = jnp.dot(
            one_hot, pool_ref[:, piece], preferred_element_type=F32
        ).astype(BF16)
    w_load.wait()
    goal_load.wait()
    base = jnp.dot(x_ref[...], w_ref[...], preferred_element_type=F32) * inv_width

    overlaps = {}
    for s in range(0, STEPS - 1, 2):
        stop = min(s + 2, STEPS - 1)
        overlaps[s] = contract(
            x_ref[(s + 1) * batch :, :], x_ref[s * batch : stop * batch, :], ((1,), (1,))
        )

    spread = []
    for s in range(STEPS - 1):
        first = s // 2 * 2
        halves = []
        for t in range(s + 1, STEPS):
            down, across = (t - first - 1) * batch, (s - first) * batch
            block = overlaps[first][down : down + batch, across : across + batch]
            block = block * (reach(t - s) * inv_batch * inv_width)
            high = block.astype(BF16)
            halves += [high, (block - high.astype(F32)).astype(BF16)]
        spread.append(jnp.concatenate(halves, axis=0))

    hidden = [base[t * batch : (t + 1) * batch] for t in range(STEPS)]
    final = []
    for s in range(STEPS):
        sigma = jax.nn.sigmoid(hidden[s])
        wanted = goal_ref[s * batch : (s + 1) * batch, :].astype(F32)
        grad = (hidden[s] * sigma - wanted) * (sigma * (1.0 + hidden[s] * (1.0 - sigma)))
        if s < STEPS - 1:
            moved = jnp.dot(spread[s], grad.astype(BF16), preferred_element_type=F32)
            for n, t in enumerate(range(s + 1, STEPS)):
                at = 2 * n * batch
                hidden[t] = hidden[t] - (
                    moved[at : at + batch] + moved[at + batch : at + 2 * batch]
                )
        final.append((grad * (-reach(STEPS - s) * inv_batch)).T.astype(BF16))

    turned_ref[...] = jnp.concatenate(final, axis=1)
    share_rows(turned_ref, x_ref, partner, first_ref)
    start = pl.multiple_of(lax.axis_index("rep") * seg, seg)
    own_ref[...] = w_ref[pl.ds(start, seg), :]


def distances(parts):
    def far(distance):
        return (distance == 1, distance & 1, -(distance >> 1).bit_count(), distance)

    return [0, *sorted(range(1, parts), key=far)]


def pair_list(count):
    return [(i, j) for i in range(count) for j in range(i, count)]


def gram_kernel(parts, order, known, *refs):
    count = len(order)
    deltas, before, out_ref = refs[:count], refs[count:-1], refs[-1]
    rows, seg = deltas[0].shape
    lanes = min(128, seg)
    block = min(8, count)
    tall = 16
    me = lax.axis_index("rep")
    down = lax.broadcasted_iota(jnp.int32, out_ref.shape, 0)
    spots = down * 128 + lax.broadcasted_iota(jnp.int32, out_ref.shape, 1)
    table = before[0][...] if before else jnp.zeros(out_ref.shape, F32)
    for first in range(0, count, block):
        for second in range(first, count, block):
            pairs = [
                (i, j)
                for i in range(first, min(first + block, count))
                for j in range(second, min(second + block, count))
                if i <= j and j >= known
            ]
            if not pairs:
                continue
            members = sorted({k for pair in pairs for k in pair})

            def step(at, sums, pairs=pairs, members=members):
                sums = list(sums)
                row = pl.multiple_of(at * tall, tall)
                for lane in range(0, seg, lanes):
                    held = {
                        k: deltas[k][pl.ds(row, tall), lane : lane + lanes].astype(F32)
                        for k in members
                    }
                    for n, (i, j) in enumerate(pairs):
                        product = held[i] * held[j]
                        sums[n] = sums[n] + (product[:8] + product[8:])
                return tuple(sums)

            zeros = tuple(jnp.zeros((8, lanes), F32) for _ in pairs)
            sums = lax.fori_loop(0, rows // tall, step, zeros, unroll=4 if count <= block else 1)
            for n, (i, j) in enumerate(pairs):
                value = jnp.sum(jnp.sum(sums[n], axis=0, keepdims=True), axis=1, keepdims=True)
                mine, other = me ^ order[i], me ^ order[j]
                here = (spots == mine * parts + other) | (spots == other * parts + mine)
                table = jnp.where(here, value, table)
    out_ref[...] = table


def tree_weights(gram, count):
    weights = [None] * count
    current = dict(gram)
    width = 1
    while count > 1:
        left, right = [], []
        for i in range(0, count, 2):
            cross = current[i, i + 1]
            left_square = jnp.maximum(current[i, i], 0.0)
            right_square = jnp.maximum(current[i + 1, i + 1], 0.0)
            left.append(1.0 - cross / (2.0 * (left_square + EPSILON)))
            right.append(1.0 - cross / (2.0 * (right_square + EPSILON)))
        for i in range(count):
            scale = (right if i % 2 else left)[i // 2]
            for k in range(i * width, (i + 1) * width):
                weights[k] = scale if weights[k] is None else weights[k] * scale
        merged = {}
        for i in range(count // 2):
            for j in range(i, count // 2):

                def entry(a, b):
                    return current[min(a, b), max(a, b)]

                merged[i, j] = left[i] * (
                    left[j] * entry(2 * i, 2 * j) + right[j] * entry(2 * i, 2 * j + 1)
                ) + right[i] * (
                    left[j] * entry(2 * i + 1, 2 * j) + right[j] * entry(2 * i + 1, 2 * j + 1)
                )
        current = merged
        count //= 2
        width *= 2
    return weights


def combine_kernel(gram_ref, own_ref, *rest):
    deltas, out_ref = rest[:-1], rest[-1]
    count = len(deltas)
    me = lax.axis_index("rep")
    table = gram_ref[0]
    for member in range(1, gram_ref.shape[0]):
        table = table + gram_ref[member]
    gram = {}
    for i, j in pair_list(count):
        down, across = divmod(i * count + j, 128)
        gram[i, j] = table[down : down + 1, across : across + 1]
    weights = tree_weights(gram, count)
    total = None
    for distance, delta in zip(distances(count), deltas):
        weight = weights[0]
        for k in range(1, count):
            weight = jnp.where((me ^ distance) == k, weights[k], weight)
        term = weight * delta[...].astype(F32)
        total = term if total is None else total + term
    combined = total.T.astype(BF16).astype(F32)
    out_ref[...] = (own_ref[...].astype(F32) + combined).astype(BF16)


def place_kernel(routes, *refs):
    pieces, (out_ref, sems) = refs[:-2], refs[-2:]
    seg = pieces[0].shape[0]
    me = lax.axis_index("rep")
    moves = []
    for n, ((even, odd), piece) in enumerate(zip(routes, pieces)):
        distance = jnp.where(me % 2 == 1, odd, even)
        at = pl.multiple_of((me ^ distance) * seg, seg)
        move = pltpu.make_async_copy(piece, out_ref.at[pl.ds(at, seg)], sems.at[n])
        move.start()
        moves.append(move)
    for move in moves:
        move.wait()


def call(kernel, out_shape, in_specs, scratch=(), out_specs=None):
    extra = {} if out_specs is None else {"out_specs": out_specs}
    return pl.pallas_call(
        kernel,
        out_shape=out_shape,
        in_specs=in_specs,
        scratch_shapes=scratch,
        compiler_params=pltpu.CompilerParams(vmem_limit_bytes=VMEM_LIMIT),
        **extra,
    )


def hold(value):
    return pltpu.with_memory_space_constraint(value, pltpu.HBM)


def flipped(value, replica_bits, shard_bits=0):
    replicas, shards = lax.axis_size("rep"), lax.axis_size("shard")
    bits = replica_bits if isinstance(replica_bits, tuple) else (replica_bits,) * 2
    pairs = [
        (i * shards + j, (i ^ bits[i % 2]) * shards + (j ^ shard_bits))
        for i in range(replicas)
        for j in range(shards)
    ]
    return lax.ppermute(value, ("rep", "shard"), pairs)


def body(token_pool, row_index, weights, targets):
    parts = lax.axis_size("rep")
    width, columns = weights.shape[1:]
    cut = FF // columns
    seg = width // parts
    rows = row_index.shape[-1]
    pool_rows = token_pool.shape[1]
    near = pl.BlockSpec(memory_space=pltpu.VMEM)
    far = pl.BlockSpec(memory_space=pltpu.HBM)
    any_place = pl.BlockSpec(memory_space=pl.ANY)

    order = distances(parts)
    first = order[1]

    def local(*refs):
        local_kernel(cut, first, *refs)

    rows_out = jax.ShapeDtypeStruct((columns, seg), BF16)
    out, own_weights, turned, gathered = call(
        local,
        [
            rows_out,
            jax.ShapeDtypeStruct((seg, columns), BF16),
            jax.ShapeDtypeStruct((columns, rows), BF16),
            jax.ShapeDtypeStruct((rows, width), BF16),
        ],
        [far] * 4,
        [
            pltpu.VMEM((1, rows), jnp.int32),
            pltpu.VMEM((pool_rows, width), BF16),
            pltpu.VMEM((width, columns), BF16),
            pltpu.VMEM((rows, columns), BF16),
            pltpu.SemaphoreType.DMA((LOADS + 3,)),
        ],
    )(hold(row_index[0]), hold(token_pool[0]), hold(weights[0]), hold(targets[0, 0]))
    leaves = {first: flipped(out, first)}
    middle = max(2, parts - 2)
    for group, after in (
        ([0, *order[2:middle]], []),
        (order[middle:], [leaves[first]]),
    ):
        if not group:
            continue

        def shares(*refs, group=group):
            share_kernel(group, *refs)

        made = call(shares, [rows_out] * len(group), [near] * (2 + len(after)))(
            turned, gathered, *after
        )
        for d, out in zip(group, made):
            leaves[d] = flipped(out, d) if d else out

    table = jax.ShapeDtypeStruct((-(-parts * parts // 128), 128), F32)
    gram, known = [], 0
    for reached in (parts - 3, parts):
        if reached <= known:
            continue
        taken = order[:reached]

        def products(*refs, taken=taken, known=known):
            gram_kernel(parts, taken, known, *refs)

        inputs = [leaves[d] for d in taken] + gram
        gram, known = [call(products, table, [near] * len(inputs))(*inputs)], reached
    gram = gram[0]
    shards = lax.axis_size("shard")
    groups = [
        [i * shards + j for i in range(parts) for j in range(first, first + cut)]
        for first in range(0, shards, cut)
    ]
    groups = [group[::-1] for group in groups]
    gram = jnp.broadcast_to(gram, (parts * cut, *gram.shape))
    gram = lax.all_to_all(gram, ("rep", "shard"), 0, 0, axis_index_groups=groups)

    own = call(
        combine_kernel,
        jax.ShapeDtypeStruct((seg, columns), BF16),
        [near] * (parts + 2),
    )(gram, own_weights, *(leaves[d] for d in order))
    pieces = {(0, 0): own, (1, 1): flipped(own, 1)}
    bits = parts.bit_length() - 2
    for chip in range(parts // 2 - 1, 0, -1):
        mirror = sum((chip >> k & 1) << (bits - 1 - k) for k in range(bits))
        if mirror == chip:
            came, passed = (2 * chip + 1, 2 * chip + 1), (2 * chip, 2 * chip)
        else:
            came, passed = (2 * chip, 2 * mirror), (2 * mirror + 1, 2 * chip + 1)
        pieces[came] = flipped(own, came)
        pieces[passed] = flipped(pieces[came], 1)

    def place(*refs):
        place_kernel(list(pieces), *refs)

    placed = call(
        place,
        jax.ShapeDtypeStruct((width, columns), BF16),
        [any_place] * parts,
        [pltpu.SemaphoreType.DMA((parts,))],
        far,
    )(*pieces.values())
    return placed[None]


def solution(mesh):
    in_specs = (
        P("rep", None, None),
        P("rep", None, None, None),
        P(None, None, "shard"),
        P("rep", None, None, "shard"),
    )
    out_specs = P(None, None, "shard")
    return jax.shard_map(body, mesh=mesh, in_specs=in_specs, out_specs=out_specs, check_vma=False)
```

```python
import math

import jax
import jax.numpy as jnp
from jax import lax
from jax.experimental import pallas as pl
from jax.experimental.pallas import tpu as pltpu
from jax.sharding import PartitionSpec as P

FF = 512
STEPS = 4
LEARN_RATE = 0.3
MOMENTUM = 0.9
EPSILON = 1e-06
LOADS = 4
VMEM_LIMIT = 48 * 1024 * 1024

F32 = jnp.float32
BF16 = jnp.bfloat16


def reach(steps_between):
    return LEARN_RATE * sum(MOMENTUM**k for k in range(steps_between))


def contract(a, b, dims):
    return lax.dot_general(a, b, (dims, ((), ())), preferred_element_type=F32)


def share_rows(turned_ref, x_ref, distance, out_ref):
    seg = out_ref.shape[1]
    target = lax.axis_index("rep") ^ distance
    held = max(seg, 128)
    at = pl.multiple_of(target * seg // held * held, held)
    moved = jnp.dot(turned_ref[...], x_ref[:, pl.ds(at, held)], preferred_element_type=F32)
    share = moved[:, :seg]
    for place in range(1, held // seg):
        own = target % (held // seg) == place
        share = jnp.where(own, moved[:, place * seg : (place + 1) * seg], share)
    out_ref[...] = share.astype(BF16)


def share_kernel(order, turned_ref, x_ref, *rest):
    for distance, out_ref in zip(order, rest[-len(order) :]):
        share_rows(turned_ref, x_ref, distance, out_ref)


def local_kernel(cut, partner, idx_hbm, pool_hbm, w_hbm, goal_hbm, *rest):
    first_ref, own_ref, turned_ref, x_ref = rest[:4]
    idx_ref, pool_ref, w_ref, goal_ref, sems = rest[4:]
    pool_rows, width = pool_ref.shape
    seg = own_ref.shape[0]
    total_rows = idx_ref.shape[-1]
    batch = total_rows // STEPS
    inv_width = 1.0 / math.sqrt(width)
    inv_batch = 1.0 / math.sqrt(batch)
    share = width // LOADS
    pieces = [pl.ds(n * share, share) for n in range(LOADS)]

    idx_load = pltpu.make_async_copy(
        idx_hbm.at[lax.axis_index("shard") // cut], idx_ref, sems.at[len(pieces) + 2]
    )
    idx_load.start()
    pool_loads = []
    for n in range(LOADS):
        rows = pl.ds(n * (pool_rows // LOADS), pool_rows // LOADS)
        load = pltpu.make_async_copy(pool_hbm.at[rows], pool_ref.at[rows], sems.at[n])
        load.start()
        pool_loads.append(load)
    w_load = pltpu.make_async_copy(w_hbm, w_ref, sems.at[len(pieces)])
    goal_load = pltpu.make_async_copy(goal_hbm, goal_ref, sems.at[len(pieces) + 1])

    idx_load.wait()
    place = lax.broadcasted_iota(jnp.int32, (batch, pool_rows), 1)
    hits = []
    for t in range(STEPS):
        picked = jnp.broadcast_to(idx_ref[:, t * batch : (t + 1) * batch], (8, batch))
        picked = picked.astype(F32).T[:, :1].astype(jnp.int32)
        hits.append(jnp.where(place == picked, 1.0, 0.0).astype(BF16))
    one_hot = jnp.concatenate(hits, axis=0)
    pool_loads[0].wait()
    w_load.start()
    goal_load.start()
    for load in pool_loads[1:]:
        load.wait()
    for piece in pieces:
        x_ref[:, piece] = jnp.dot(
            one_hot, pool_ref[:, piece], preferred_element_type=F32
        ).astype(BF16)
    w_load.wait()
    goal_load.wait()
    base = jnp.dot(x_ref[...], w_ref[...], preferred_element_type=F32) * inv_width

    overlaps = {}
    for s in range(0, STEPS - 1, 2):
        stop = min(s + 2, STEPS - 1)
        overlaps[s] = contract(
            x_ref[(s + 1) * batch :, :], x_ref[s * batch : stop * batch, :], ((1,), (1,))
        )

    spread = []
    for s in range(STEPS - 1):
        first = s // 2 * 2
        halves = []
        for t in range(s + 1, STEPS):
            down, across = (t - first - 1) * batch, (s - first) * batch
            block = overlaps[first][down : down + batch, across : across + batch]
            block = block * (reach(t - s) * inv_batch * inv_width)
            high = block.astype(BF16)
            halves += [high, (block - high.astype(F32)).astype(BF16)]
        spread.append(jnp.concatenate(halves, axis=0))

    hidden = [base[t * batch : (t + 1) * batch] for t in range(STEPS)]
    final = []
    for s in range(STEPS):
        sigma = jax.nn.sigmoid(hidden[s])
        wanted = goal_ref[s * batch : (s + 1) * batch, :].astype(F32)
        grad = (hidden[s] * sigma - wanted) * (sigma * (1.0 + hidden[s] * (1.0 - sigma)))
        if s < STEPS - 1:
            moved = jnp.dot(spread[s], grad.astype(BF16), preferred_element_type=F32)
            for n, t in enumerate(range(s + 1, STEPS)):
                at = 2 * n * batch
                hidden[t] = hidden[t] - (
                    moved[at : at + batch] + moved[at + batch : at + 2 * batch]
                )
        final.append((grad * (-reach(STEPS - s) * inv_batch)).T.astype(BF16))

    turned_ref[...] = jnp.concatenate(final, axis=1)
    share_rows(turned_ref, x_ref, partner, first_ref)
    start = pl.multiple_of(lax.axis_index("rep") * seg, seg)
    own_ref[...] = w_ref[pl.ds(start, seg), :]


def distances(parts):
    def far(distance):
        return (distance == 1, distance & 1, -(distance >> 1).bit_count(), distance)

    return [0, *sorted(range(1, parts), key=far)]


def pair_list(count):
    return [(i, j) for i in range(count) for j in range(i, count)]


def gram_kernel(parts, order, known, *refs):
    count = len(order)
    deltas, before, out_ref = refs[:count], refs[count:-1], refs[-1]
    rows, seg = deltas[0].shape
    lanes = min(128, seg)
    block = min(8, count)
    tall = 16
    me = lax.axis_index("rep")
    down = lax.broadcasted_iota(jnp.int32, out_ref.shape, 0)
    spots = down * 128 + lax.broadcasted_iota(jnp.int32, out_ref.shape, 1)
    table = before[0][...] if before else jnp.zeros(out_ref.shape, F32)
    for first in range(0, count, block):
        for second in range(first, count, block):
            pairs = [
                (i, j)
                for i in range(first, min(first + block, count))
                for j in range(second, min(second + block, count))
                if i <= j and j >= known
            ]
            if not pairs:
                continue
            members = sorted({k for pair in pairs for k in pair})

            def step(at, sums, pairs=pairs, members=members):
                sums = list(sums)
                row = pl.multiple_of(at * tall, tall)
                for lane in range(0, seg, lanes):
                    held = {
                        k: deltas[k][pl.ds(row, tall), lane : lane + lanes].astype(F32)
                        for k in members
                    }
                    for n, (i, j) in enumerate(pairs):
                        product = held[i] * held[j]
                        sums[n] = sums[n] + (product[:8] + product[8:])
                return tuple(sums)

            zeros = tuple(jnp.zeros((8, lanes), F32) for _ in pairs)
            sums = lax.fori_loop(0, rows // tall, step, zeros, unroll=4 if count <= block else 1)
            for n, (i, j) in enumerate(pairs):
                value = jnp.sum(jnp.sum(sums[n], axis=0, keepdims=True), axis=1, keepdims=True)
                mine, other = me ^ order[i], me ^ order[j]
                here = (spots == mine * parts + other) | (spots == other * parts + mine)
                table = jnp.where(here, value, table)
    out_ref[...] = table


def tree_weights(gram, count):
    weights = [None] * count
    current = dict(gram)
    width = 1
    while count > 1:
        left, right = [], []
        for i in range(0, count, 2):
            cross = current[i, i + 1]
            left_square = jnp.maximum(current[i, i], 0.0)
            right_square = jnp.maximum(current[i + 1, i + 1], 0.0)
            left.append(1.0 - cross / (2.0 * (left_square + EPSILON)))
            right.append(1.0 - cross / (2.0 * (right_square + EPSILON)))
        for i in range(count):
            scale = (right if i % 2 else left)[i // 2]
            for k in range(i * width, (i + 1) * width):
                weights[k] = scale if weights[k] is None else weights[k] * scale
        merged = {}
        for i in range(count // 2):
            for j in range(i, count // 2):

                def entry(a, b):
                    return current[min(a, b), max(a, b)]

                merged[i, j] = left[i] * (
                    left[j] * entry(2 * i, 2 * j) + right[j] * entry(2 * i, 2 * j + 1)
                ) + right[i] * (
                    left[j] * entry(2 * i + 1, 2 * j) + right[j] * entry(2 * i + 1, 2 * j + 1)
                )
        current = merged
        count //= 2
        width *= 2
    return weights


def combine_kernel(gram_ref, own_ref, *rest):
    deltas, out_ref = rest[:-1], rest[-1]
    count = len(deltas)
    me = lax.axis_index("rep")
    table = gram_ref[0]
    for member in range(1, gram_ref.shape[0]):
        table = table + gram_ref[member]
    gram = {}
    for i, j in pair_list(count):
        down, across = divmod(i * count + j, 128)
        gram[i, j] = table[down : down + 1, across : across + 1]
    weights = tree_weights(gram, count)
    total = None
    for distance, delta in zip(distances(count), deltas):
        weight = weights[0]
        for k in range(1, count):
            weight = jnp.where((me ^ distance) == k, weights[k], weight)
        term = weight * delta[...].astype(F32)
        total = term if total is None else total + term
    combined = total.T.astype(BF16).astype(F32)
    out_ref[...] = (own_ref[...].astype(F32) + combined).astype(BF16)


def place_kernel(routes, *refs):
    pieces, (out_ref, sems) = refs[:-2], refs[-2:]
    seg = pieces[0].shape[0]
    me = lax.axis_index("rep")
    moves = []
    for n, ((even, odd), piece) in enumerate(zip(routes, pieces)):
        distance = jnp.where(me % 2 == 1, odd, even)
        at = pl.multiple_of((me ^ distance) * seg, seg)
        move = pltpu.make_async_copy(piece, out_ref.at[pl.ds(at, seg)], sems.at[n])
        move.start()
        moves.append(move)
    for move in moves:
        move.wait()


def call(kernel, out_shape, in_specs, scratch=(), out_specs=None):
    extra = {} if out_specs is None else {"out_specs": out_specs}
    return pl.pallas_call(
        kernel,
        out_shape=out_shape,
        in_specs=in_specs,
        scratch_shapes=scratch,
        compiler_params=pltpu.CompilerParams(vmem_limit_bytes=VMEM_LIMIT),
        **extra,
    )


def hold(value):
    return pltpu.with_memory_space_constraint(value, pltpu.HBM)


def flipped(value, replica_bits, shard_bits=0):
    replicas, shards = lax.axis_size("rep"), lax.axis_size("shard")
    bits = replica_bits if isinstance(replica_bits, tuple) else (replica_bits,) * 2
    pairs = [
        (i * shards + j, (i ^ bits[i % 2]) * shards + (j ^ shard_bits))
        for i in range(replicas)
        for j in range(shards)
    ]
    return lax.ppermute(value, ("rep", "shard"), pairs)


def body(token_pool, row_index, weights, targets):
    parts = lax.axis_size("rep")
    width, columns = weights.shape[1:]
    cut = FF // columns
    seg = width // parts
    rows = row_index.shape[-1]
    pool_rows = token_pool.shape[1]
    near = pl.BlockSpec(memory_space=pltpu.VMEM)
    far = pl.BlockSpec(memory_space=pltpu.HBM)
    any_place = pl.BlockSpec(memory_space=pl.ANY)

    order = distances(parts)
    first = order[1]

    def local(*refs):
        local_kernel(cut, first, *refs)

    rows_out = jax.ShapeDtypeStruct((columns, seg), BF16)
    out, own_weights, turned, gathered = call(
        local,
        [
            rows_out,
            jax.ShapeDtypeStruct((seg, columns), BF16),
            jax.ShapeDtypeStruct((columns, rows), BF16),
            jax.ShapeDtypeStruct((rows, width), BF16),
        ],
        [far] * 4,
        [
            pltpu.VMEM((1, rows), jnp.int32),
            pltpu.VMEM((pool_rows, width), BF16),
            pltpu.VMEM((width, columns), BF16),
            pltpu.VMEM((rows, columns), BF16),
            pltpu.SemaphoreType.DMA((LOADS + 3,)),
        ],
    )(hold(row_index[0]), hold(token_pool[0]), hold(weights[0]), hold(targets[0, 0]))
    leaves = {first: flipped(out, first)}
    middle = max(2, parts - 1)
    for group, after in (
        ([0, *order[2:middle]], []),
        (order[middle:], [leaves[first]]),
    ):
        if not group:
            continue

        def shares(*refs, group=group):
            share_kernel(group, *refs)

        made = call(shares, [rows_out] * len(group), [near] * (2 + len(after)))(
            turned, gathered, *after
        )
        for d, out in zip(group, made):
            leaves[d] = flipped(out, d) if d else out

    table = jax.ShapeDtypeStruct((-(-parts * parts // 128), 128), F32)
    gram, known = [], 0
    for reached in (parts - 3, parts - 2, parts):
        if reached <= known:
            continue
        taken = order[:reached]

        def products(*refs, taken=taken, known=known):
            gram_kernel(parts, taken, known, *refs)

        inputs = [leaves[d] for d in taken] + gram
        gram, known = [call(products, table, [near] * len(inputs))(*inputs)], reached
    gram = gram[0]
    shards = lax.axis_size("shard")
    groups = [
        [i * shards + j for i in range(parts) for j in range(first, first + cut)]
        for first in range(0, shards, cut)
    ]
    groups = [group[::-1] for group in groups]
    gram = jnp.broadcast_to(gram, (parts * cut, *gram.shape))
    gram = lax.all_to_all(gram, ("rep", "shard"), 0, 0, axis_index_groups=groups)

    own = call(
        combine_kernel,
        jax.ShapeDtypeStruct((seg, columns), BF16),
        [near] * (parts + 2),
    )(gram, own_weights, *(leaves[d] for d in order))
    pieces = {(0, 0): own, (1, 1): flipped(own, 1)}
    bits = parts.bit_length() - 2
    for chip in range(parts // 2 - 1, 0, -1):
        mirror = sum((chip >> k & 1) << (bits - 1 - k) for k in range(bits))
        if mirror == chip:
            came, passed = (2 * chip + 1, 2 * chip + 1), (2 * chip, 2 * chip)
        else:
            came, passed = (2 * chip, 2 * mirror), (2 * mirror + 1, 2 * chip + 1)
        pieces[came] = flipped(own, came)
        pieces[passed] = flipped(pieces[came], 1)

    def place(*refs):
        place_kernel(list(pieces), *refs)

    placed = call(
        place,
        jax.ShapeDtypeStruct((width, columns), BF16),
        [any_place] * parts,
        [pltpu.SemaphoreType.DMA((parts,))],
        far,
    )(*pieces.values())
    return placed[None]


def solution(mesh):
    in_specs = (
        P("rep", None, None),
        P("rep", None, None, None),
        P(None, None, "shard"),
        P("rep", None, None, "shard"),
    )
    out_specs = P(None, None, "shard")
    return jax.shard_map(body, mesh=mesh, in_specs=in_specs, out_specs=out_specs, check_vma=False)
```

```python
import math

import jax
import jax.numpy as jnp
from jax import lax
from jax.experimental import pallas as pl
from jax.experimental.pallas import tpu as pltpu
from jax.sharding import PartitionSpec as P

FF = 512
STEPS = 4
LEARN_RATE = 0.3
MOMENTUM = 0.9
EPSILON = 1e-06
LOADS = 4
VMEM_LIMIT = 48 * 1024 * 1024

F32 = jnp.float32
BF16 = jnp.bfloat16


def reach(steps_between):
    return LEARN_RATE * sum(MOMENTUM**k for k in range(steps_between))


def contract(a, b, dims):
    return lax.dot_general(a, b, (dims, ((), ())), preferred_element_type=F32)


def share_rows(turned_ref, x_ref, distance, out_ref):
    seg = out_ref.shape[1]
    target = lax.axis_index("rep") ^ distance
    held = max(seg, 128)
    at = pl.multiple_of(target * seg // held * held, held)
    moved = jnp.dot(turned_ref[...], x_ref[:, pl.ds(at, held)], preferred_element_type=F32)
    share = moved[:, :seg]
    for place in range(1, held // seg):
        own = target % (held // seg) == place
        share = jnp.where(own, moved[:, place * seg : (place + 1) * seg], share)
    out_ref[...] = share.astype(BF16)


def share_kernel(order, turned_ref, x_ref, *rest):
    for distance, out_ref in zip(order, rest[-len(order) :]):
        share_rows(turned_ref, x_ref, distance, out_ref)


def local_kernel(cut, partner, idx_hbm, pool_hbm, w_hbm, goal_hbm, *rest):
    first_ref, own_ref, turned_ref, x_ref = rest[:4]
    idx_ref, pool_ref, w_ref, goal_ref, sems = rest[4:]
    pool_rows, width = pool_ref.shape
    seg = own_ref.shape[0]
    total_rows = idx_ref.shape[-1]
    batch = total_rows // STEPS
    inv_width = 1.0 / math.sqrt(width)
    inv_batch = 1.0 / math.sqrt(batch)
    share = width // LOADS
    pieces = [pl.ds(n * share, share) for n in range(LOADS)]

    idx_load = pltpu.make_async_copy(
        idx_hbm.at[lax.axis_index("shard") // cut], idx_ref, sems.at[len(pieces) + 2]
    )
    idx_load.start()
    pool_loads = []
    for n in range(LOADS):
        rows = pl.ds(n * (pool_rows // LOADS), pool_rows // LOADS)
        load = pltpu.make_async_copy(pool_hbm.at[rows], pool_ref.at[rows], sems.at[n])
        load.start()
        pool_loads.append(load)
    w_load = pltpu.make_async_copy(w_hbm, w_ref, sems.at[len(pieces)])
    goal_load = pltpu.make_async_copy(goal_hbm, goal_ref, sems.at[len(pieces) + 1])

    idx_load.wait()
    place = lax.broadcasted_iota(jnp.int32, (batch, pool_rows), 1)
    hits = []
    for t in range(STEPS):
        picked = jnp.broadcast_to(idx_ref[:, t * batch : (t + 1) * batch], (8, batch))
        picked = picked.astype(F32).T[:, :1].astype(jnp.int32)
        hits.append(jnp.where(place == picked, 1.0, 0.0).astype(BF16))
    one_hot = jnp.concatenate(hits, axis=0)
    pool_loads[0].wait()
    w_load.start()
    goal_load.start()
    for load in pool_loads[1:]:
        load.wait()
    for piece in pieces:
        x_ref[:, piece] = jnp.dot(
            one_hot, pool_ref[:, piece], preferred_element_type=F32
        ).astype(BF16)
    w_load.wait()
    goal_load.wait()
    base = jnp.dot(x_ref[...], w_ref[...], preferred_element_type=F32) * inv_width

    overlaps = {}
    for s in range(0, STEPS - 1, 2):
        stop = min(s + 2, STEPS - 1)
        overlaps[s] = contract(
            x_ref[(s + 1) * batch :, :], x_ref[s * batch : stop * batch, :], ((1,), (1,))
        )

    spread = []
    for s in range(STEPS - 1):
        first = s // 2 * 2
        halves = []
        for t in range(s + 1, STEPS):
            down, across = (t - first - 1) * batch, (s - first) * batch
            block = overlaps[first][down : down + batch, across : across + batch]
            block = block * (reach(t - s) * inv_batch * inv_width)
            high = block.astype(BF16)
            halves += [high, (block - high.astype(F32)).astype(BF16)]
        spread.append(jnp.concatenate(halves, axis=0))

    hidden = [base[t * batch : (t + 1) * batch] for t in range(STEPS)]
    final = []
    for s in range(STEPS):
        sigma = jax.nn.sigmoid(hidden[s])
        wanted = goal_ref[s * batch : (s + 1) * batch, :].astype(F32)
        grad = (hidden[s] * sigma - wanted) * (sigma * (1.0 + hidden[s] * (1.0 - sigma)))
        if s < STEPS - 1:
            moved = jnp.dot(spread[s], grad.astype(BF16), preferred_element_type=F32)
            for n, t in enumerate(range(s + 1, STEPS)):
                at = 2 * n * batch
                hidden[t] = hidden[t] - (
                    moved[at : at + batch] + moved[at + batch : at + 2 * batch]
                )
        final.append((grad * (-reach(STEPS - s) * inv_batch)).T.astype(BF16))

    turned_ref[...] = jnp.concatenate(final, axis=1)
    share_rows(turned_ref, x_ref, partner, first_ref)
    start = pl.multiple_of(lax.axis_index("rep") * seg, seg)
    own_ref[...] = w_ref[pl.ds(start, seg), :]


def distances(parts):
    def far(distance):
        return (distance == 1, distance & 1, -(distance >> 1).bit_count(), distance)

    return [0, *sorted(range(1, parts), key=far)]


def pair_list(count):
    return [(i, j) for i in range(count) for j in range(i, count)]


def gram_kernel(parts, order, known, *refs):
    count = len(order)
    deltas, before, out_ref = refs[:count], refs[count:-1], refs[-1]
    rows, seg = deltas[0].shape
    lanes = min(128, seg)
    block = min(8, count)
    tall = 16
    me = lax.axis_index("rep")
    down = lax.broadcasted_iota(jnp.int32, out_ref.shape, 0)
    spots = down * 128 + lax.broadcasted_iota(jnp.int32, out_ref.shape, 1)
    table = before[0][...] if before else jnp.zeros(out_ref.shape, F32)
    for first in range(0, count, block):
        for second in range(first, count, block):
            pairs = [
                (i, j)
                for i in range(first, min(first + block, count))
                for j in range(second, min(second + block, count))
                if i <= j and j >= known
            ]
            if not pairs:
                continue
            members = sorted({k for pair in pairs for k in pair})

            def step(at, sums, pairs=pairs, members=members):
                sums = list(sums)
                row = pl.multiple_of(at * tall, tall)
                for lane in range(0, seg, lanes):
                    held = {
                        k: deltas[k][pl.ds(row, tall), lane : lane + lanes].astype(F32)
                        for k in members
                    }
                    for n, (i, j) in enumerate(pairs):
                        product = held[i] * held[j]
                        sums[n] = sums[n] + (product[:8] + product[8:])
                return tuple(sums)

            zeros = tuple(jnp.zeros((8, lanes), F32) for _ in pairs)
            sums = lax.fori_loop(0, rows // tall, step, zeros, unroll=4 if count <= block else 1)
            for n, (i, j) in enumerate(pairs):
                value = jnp.sum(jnp.sum(sums[n], axis=0, keepdims=True), axis=1, keepdims=True)
                mine, other = me ^ order[i], me ^ order[j]
                here = (spots == mine * parts + other) | (spots == other * parts + mine)
                table = jnp.where(here, value, table)
    out_ref[...] = table


def tree_weights(gram, count):
    weights = [None] * count
    current = dict(gram)
    width = 1
    while count > 1:
        left, right = [], []
        for i in range(0, count, 2):
            cross = current[i, i + 1]
            left_square = jnp.maximum(current[i, i], 0.0)
            right_square = jnp.maximum(current[i + 1, i + 1], 0.0)
            left.append(1.0 - cross / (2.0 * (left_square + EPSILON)))
            right.append(1.0 - cross / (2.0 * (right_square + EPSILON)))
        for i in range(count):
            scale = (right if i % 2 else left)[i // 2]
            for k in range(i * width, (i + 1) * width):
                weights[k] = scale if weights[k] is None else weights[k] * scale
        merged = {}
        for i in range(count // 2):
            for j in range(i, count // 2):

                def entry(a, b):
                    return current[min(a, b), max(a, b)]

                merged[i, j] = left[i] * (
                    left[j] * entry(2 * i, 2 * j) + right[j] * entry(2 * i, 2 * j + 1)
                ) + right[i] * (
                    left[j] * entry(2 * i + 1, 2 * j) + right[j] * entry(2 * i + 1, 2 * j + 1)
                )
        current = merged
        count //= 2
        width *= 2
    return weights


def combine_kernel(gram_ref, own_ref, *rest):
    deltas, out_ref = rest[:-1], rest[-1]
    count = len(deltas)
    me = lax.axis_index("rep")
    table = gram_ref[0]
    for member in range(1, gram_ref.shape[0]):
        table = table + gram_ref[member]
    gram = {}
    for i, j in pair_list(count):
        down, across = divmod(i * count + j, 128)
        gram[i, j] = table[down : down + 1, across : across + 1]
    weights = tree_weights(gram, count)
    total = None
    for distance, delta in zip(distances(count), deltas):
        weight = weights[0]
        for k in range(1, count):
            weight = jnp.where((me ^ distance) == k, weights[k], weight)
        term = weight * delta[...].astype(F32)
        total = term if total is None else total + term
    combined = total.astype(BF16).T.astype(F32)
    out_ref[...] = (own_ref[...].astype(F32) + combined).astype(BF16)


def place_kernel(routes, *refs):
    pieces, (out_ref, sems) = refs[:-2], refs[-2:]
    seg = pieces[0].shape[0]
    me = lax.axis_index("rep")
    moves = []
    for n, ((even, odd), piece) in enumerate(zip(routes, pieces)):
        distance = jnp.where(me % 2 == 1, odd, even)
        at = pl.multiple_of((me ^ distance) * seg, seg)
        move = pltpu.make_async_copy(piece, out_ref.at[pl.ds(at, seg)], sems.at[n])
        move.start()
        moves.append(move)
    for move in moves:
        move.wait()


def call(kernel, out_shape, in_specs, scratch=(), out_specs=None):
    extra = {} if out_specs is None else {"out_specs": out_specs}
    return pl.pallas_call(
        kernel,
        out_shape=out_shape,
        in_specs=in_specs,
        scratch_shapes=scratch,
        compiler_params=pltpu.CompilerParams(vmem_limit_bytes=VMEM_LIMIT),
        **extra,
    )


def hold(value):
    return pltpu.with_memory_space_constraint(value, pltpu.HBM)


def flipped(value, replica_bits, shard_bits=0):
    replicas, shards = lax.axis_size("rep"), lax.axis_size("shard")
    bits = replica_bits if isinstance(replica_bits, tuple) else (replica_bits,) * 2
    pairs = [
        (i * shards + j, (i ^ bits[i % 2]) * shards + (j ^ shard_bits))
        for i in range(replicas)
        for j in range(shards)
    ]
    return lax.ppermute(value, ("rep", "shard"), pairs)


def body(token_pool, row_index, weights, targets):
    parts = lax.axis_size("rep")
    width, columns = weights.shape[1:]
    cut = FF // columns
    seg = width // parts
    rows = row_index.shape[-1]
    pool_rows = token_pool.shape[1]
    near = pl.BlockSpec(memory_space=pltpu.VMEM)
    far = pl.BlockSpec(memory_space=pltpu.HBM)
    any_place = pl.BlockSpec(memory_space=pl.ANY)

    order = distances(parts)
    first = order[1]

    def local(*refs):
        local_kernel(cut, first, *refs)

    rows_out = jax.ShapeDtypeStruct((columns, seg), BF16)
    out, own_weights, turned, gathered = call(
        local,
        [
            rows_out,
            jax.ShapeDtypeStruct((seg, columns), BF16),
            jax.ShapeDtypeStruct((columns, rows), BF16),
            jax.ShapeDtypeStruct((rows, width), BF16),
        ],
        [far] * 4,
        [
            pltpu.VMEM((1, rows), jnp.int32),
            pltpu.VMEM((pool_rows, width), BF16),
            pltpu.VMEM((width, columns), BF16),
            pltpu.VMEM((rows, columns), BF16),
            pltpu.SemaphoreType.DMA((LOADS + 3,)),
        ],
    )(hold(row_index[0]), hold(token_pool[0]), hold(weights[0]), hold(targets[0, 0]))
    leaves = {first: flipped(out, first)}
    middle = max(2, parts - 1)
    for group, after in (
        ([0, *order[2:middle]], []),
        (order[middle:], [leaves[first]]),
    ):
        if not group:
            continue

        def shares(*refs, group=group):
            share_kernel(group, *refs)

        made = call(shares, [rows_out] * len(group), [near] * (2 + len(after)))(
            turned, gathered, *after
        )
        for d, out in zip(group, made):
            leaves[d] = flipped(out, d) if d else out

    table = jax.ShapeDtypeStruct((-(-parts * parts // 128), 128), F32)
    gram, known = [], 0
    for reached in (parts - 3, parts):
        if reached <= known:
            continue
        taken = order[:reached]

        def products(*refs, taken=taken, known=known):
            gram_kernel(parts, taken, known, *refs)

        inputs = [leaves[d] for d in taken] + gram
        gram, known = [call(products, table, [near] * len(inputs))(*inputs)], reached
    gram = gram[0]
    shards = lax.axis_size("shard")
    groups = [
        [i * shards + j for i in range(parts) for j in range(first, first + cut)]
        for first in range(0, shards, cut)
    ]
    groups = [group[::-1] for group in groups]
    gram = jnp.broadcast_to(gram, (parts * cut, *gram.shape))
    gram = lax.all_to_all(gram, ("rep", "shard"), 0, 0, axis_index_groups=groups)

    own = call(
        combine_kernel,
        jax.ShapeDtypeStruct((seg, columns), BF16),
        [near] * (parts + 2),
    )(gram, own_weights, *(leaves[d] for d in order))
    pieces = {(0, 0): own, (1, 1): flipped(own, 1)}
    bits = parts.bit_length() - 2
    for chip in range(parts // 2 - 1, 0, -1):
        mirror = sum((chip >> k & 1) << (bits - 1 - k) for k in range(bits))
        if mirror == chip:
            came, passed = (2 * chip + 1, 2 * chip + 1), (2 * chip, 2 * chip)
        else:
            came, passed = (2 * chip, 2 * mirror), (2 * mirror + 1, 2 * chip + 1)
        pieces[came] = flipped(own, came)
        pieces[passed] = flipped(pieces[came], 1)

    def place(*refs):
        place_kernel(list(pieces), *refs)

    placed = call(
        place,
        jax.ShapeDtypeStruct((width, columns), BF16),
        [any_place] * parts,
        [pltpu.SemaphoreType.DMA((parts,))],
        far,
    )(*pieces.values())
    return placed[None]


def solution(mesh):
    in_specs = (
        P("rep", None, None),
        P("rep", None, None, None),
        P(None, None, "shard"),
        P("rep", None, None, "shard"),
    )
    out_specs = P(None, None, "shard")
    return jax.shard_map(body, mesh=mesh, in_specs=in_specs, out_specs=out_specs, check_vma=False)
```
